512 devices in a mesh: outer: 8 (over y_hi, core), inner: 8 (over x, y_lo), tensor: 8 (over z).
Axes of the slice: x: 4, y: 8 (y_hi: 4, y_lo: 2; y = y_hi * 2 + y_lo), z: 8, core: 2. Of those that a mesh axis runs over, the one named last changes fastest.
Arguments:
- queries: bfloat16 [8192, 48, 128], P(('outer', 'inner'), 'tensor'), may hold values from -6 to 6
- keys: bfloat16 [8192, 8, 128], P(('outer', 'inner')), may hold values from -6 to 6
- values: bfloat16 [8192, 8, 128], P(('outer', 'inner')), may hold values from -6 to 6
- outputs: bfloat16 [8192, 48, 128], P(('outer', 'inner'), 'tensor'), may hold values from -6 to 6
- out_grad: bfloat16 [8192, 48, 128], P(('outer', 'inner'), 'tensor'), may hold values from -6 to 6
- log_norm: float32 [48, 8192], P('tensor', ('outer', 'inner')), may hold values from 3 to 8
- parents: int32 [64], replicated, may hold values from 0 to 62, as said below
Outputs:
- query_grad: bfloat16 [8192, 48, 128], P(('outer', 'inner'), 'tensor')
- key_grad: bfloat16 [8192, 8, 128], P(('outer', 'inner'))
- value_grad: bfloat16 [8192, 8, 128], P(('outer', 'inner'))
The draws below stay inside these ranges and needn't reach their ends.
Inputs may be any that keep to these rules, and one draw needn't show every extreme that they name: parents[b] <= b for every block b; a block with parents[b] = b starts a new rollout, every other block continues the prefix of its parent; the last block continues the block before it.
All inputs are finite; a program needn't handle non-finite values.
Results may differ from the reference program's by a relative error of at most 0.0049.
Values may be sent and summed in bfloat16 or wider, within the bound.
No kernel may reach another device: no remote copies, remote signals or barrier semaphores. Data moves between devices by JAX's collectives and lax.ppermute only.
A program may use at most 64 MiB of HBM per device.

```python
import jax
import jax.numpy as jnp
from jax import lax

HD = 128
BLK = 128
TOK_DEV = 128
QHEADS = 48
KVH = 8
TOKENS = 8192
NBLK = 64


def draw_parents(key, part):
    key = jax.random.fold_in(key, 7)
    first_key, second_key = jax.random.split(key)
    block_ids = jnp.arange(NBLK, dtype=jnp.int32)
    branch_kind = jax.random.randint(first_key, (NBLK,), 0, 10)
    earlier = jax.random.randint(second_key, (NBLK,), 0, jnp.maximum(block_ids, 1))
    previous = jnp.maximum(block_ids - 1, 0)
    parent_ids = jnp.where(branch_kind < 7, previous, jnp.where(branch_kind < 9, earlier, block_ids))
    parent_ids = jnp.where(block_ids == NBLK - 1, previous, parent_ids)
    return parent_ids.astype(jnp.int32)


def block_scale(own_key, extent, cuts, least, largest):
    loudness = 1.0
    for dim, parts in cuts:
        draws = jax.random.uniform(jax.random.fold_in(jax.random.fold_in(own_key, 6), dim), (parts,), jnp.float32, least / len(cuts), largest / len(cuts))
        loudness = loudness * jnp.repeat(jnp.exp(draws), extent[dim] // parts).reshape((-1,) + (1,) * (len(extent) - 1 - dim))
    return loudness


def bell_draw(stream_key, extent, deviation, reach, pieces=(), held_as=jnp.bfloat16):
    factor_of = block_scale(stream_key, extent, pieces, -0.22, 0.18) if pieces else 1.0
    entries = jax.random.normal(stream_key, extent, jnp.float32) * deviation * factor_of
    return jnp.minimum(jnp.maximum(entries, -reach), reach).astype(held_as)


def setup_inputs(seed: int = 0) -> dict:
    seeds = jax.random.split(jax.random.key(seed), 8)
    queries = bell_draw(seeds[0], (TOKENS, QHEADS, HD), 1.0, 6.0, ((0, 64), (1, 8)))
    keys = bell_draw(seeds[1], (TOKENS, KVH, HD), 1.0, 6.0, ((0, 64),))
    values = bell_draw(seeds[2], (TOKENS, KVH, HD), 1.0, 6.0, ((0, 64),))
    outputs = bell_draw(seeds[3], (TOKENS, QHEADS, HD), 1.0, 6.0, ((0, 64), (1, 8)))
    out_grad = bell_draw(seeds[4], (TOKENS, QHEADS, HD), 1.0, 6.0, ((0, 64), (1, 8)))
    log_norm = jnp.clip(3.0 + 5.0 * jax.random.uniform(seeds[5], (QHEADS, TOKENS), jnp.float32) ** block_scale(seeds[5], (QHEADS, TOKENS), ((0, 8), (1, 64)), -0.2, 0.2), 3.0, 8.0)
    parents = draw_parents(jax.random.fold_in(seeds[7], 71), 0)
    return dict(queries=queries, keys=keys, values=values, outputs=outputs, out_grad=out_grad, log_norm=log_norm, parents=parents)


def ancestors(parents):
    block_count = parents.shape[0]
    block_ids = jnp.arange(block_count, dtype=jnp.int32)
    reach_table = ((parents[:, None] == block_ids[None, :]) | (block_ids[:, None] == block_ids[None, :])).astype(jnp.int32)
    for rounds in range(max(block_count.bit_length(), 1)):
        reach_table = jnp.minimum(jnp.dot(reach_table, reach_table), 1)
    return reach_table


def reference(queries, keys, values, outputs, out_grad, log_norm, parents):
    token_count, head_count, head_width = queries.shape
    kv_count = keys.shape[1]
    group_size = head_count // kv_count
    scaling = head_width ** -0.5
    reach_table = ancestors(parents)
    positions = jnp.arange(token_count, dtype=jnp.int32)
    row_dots = jnp.sum(out_grad.astype(jnp.float32) * outputs.astype(jnp.float32), axis=-1)
    query_heads = jnp.moveaxis(queries, 1, 0)
    grad_heads = jnp.moveaxis(out_grad, 1, 0)
    key_heads = jnp.moveaxis(keys, 1, 0)
    value_heads = jnp.moveaxis(values, 1, 0)
    dot_heads = row_dots.T
    block_rows = TOK_DEV
    block_total = token_count // block_rows
    row_starts = jnp.arange(block_total, dtype=jnp.int32) * block_rows

    def per_head(carried, inputs):
        key_total, value_total = carried
        query_head, grad_head, norm_head, dots_head, head_index = inputs
        kv_index = head_index // group_size
        key_head = lax.dynamic_index_in_dim(key_heads, kv_index, 0, keepdims=False)
        value_head = lax.dynamic_index_in_dim(value_heads, kv_index, 0, keepdims=False)

        def per_block(block_state, row_start):
            key_acc, value_acc = block_state
            query_block = lax.dynamic_slice_in_dim(query_head, row_start, block_rows, 0)
            grad_block = lax.dynamic_slice_in_dim(grad_head, row_start, block_rows, 0)
            norm_block = lax.dynamic_slice_in_dim(norm_head, row_start, block_rows, 0)
            dots_block = lax.dynamic_slice_in_dim(dots_head, row_start, block_rows, 0)
            query_pos = row_start + jnp.arange(block_rows, dtype=jnp.int32)
            linked = reach_table[query_pos // BLK][:, positions // BLK] > 0
            allowed = linked & (query_pos[:, None] >= positions[None, :])
            scores = jnp.dot(query_block, key_head.T, preferred_element_type=jnp.float32) * scaling
            probabilities = jnp.where(allowed, jnp.exp(scores - norm_block[:, None]), jnp.float32(0.0))
            probs_low = probabilities.astype(jnp.bfloat16)
            dprobs = jnp.dot(grad_block, value_head.T, preferred_element_type=jnp.float32)
            dscores = (probabilities * (dprobs - dots_block[:, None]) * scaling).astype(jnp.bfloat16)
            query_part = jnp.dot(dscores, key_head, preferred_element_type=jnp.float32)
            key_acc = key_acc + jnp.dot(dscores.T, query_block, preferred_element_type=jnp.float32)
            value_acc = value_acc + jnp.dot(probs_low.T, grad_block, preferred_element_type=jnp.float32)
            return (key_acc, value_acc), query_part.astype(jnp.bfloat16)

        empty_rows = jnp.zeros((token_count, head_width), jnp.float32)
        (key_acc, value_acc), query_parts = lax.scan(per_block, (empty_rows, empty_rows), row_starts)
        select = (jnp.arange(kv_count, dtype=jnp.int32) == kv_index).astype(jnp.float32)[:, None, None]
        key_total = key_total + select * key_acc[None]
        value_total = value_total + select * value_acc[None]
        return (key_total, value_total), query_parts.reshape(token_count, head_width)

    empty_heads = jnp.zeros((kv_count, token_count, head_width), jnp.float32)
    head_ids = jnp.arange(head_count, dtype=jnp.int32)
    (key_total, value_total), query_parts = lax.scan(per_head, (empty_heads, empty_heads), (query_heads, grad_heads, log_norm, dot_heads, head_ids))
    query_grad = jnp.moveaxis(query_parts, 0, 1)
    key_grad = jnp.moveaxis(key_total, 0, 1).astype(jnp.bfloat16)
    value_grad = jnp.moveaxis(value_total, 0, 1).astype(jnp.bfloat16)
    return (query_grad, key_grad, value_grad)
```

```python
import functools

import jax
import jax.numpy as jnp
from jax import lax
from jax.experimental import pallas as pl
from jax.experimental.pallas import tpu as pltpu
from jax.sharding import Mesh, PartitionSpec as P

BLK = 128
HD = 128
HEADS = 6
ROWS = HEADS * BLK
NBLK = 64
KVH = 8
Y = ("yh", "yl")
STAT_ROWS = 16
PACK_ROWS = 2 * ROWS + 6 * STAT_ROWS
SCALING = HD ** -0.5
LOG2E = 1.4426950408889634
CHUNK = 2 * BLK
F32 = jnp.float32
BF16 = jnp.bfloat16


def shift(block, axis, distance):
    size = lax.axis_size(axis)
    return lax.ppermute(block, axis, [(i, (i + distance) % size) for i in range(size)])


def vmem(count):
    return [pl.BlockSpec(memory_space=pltpu.VMEM)] * count


def smem(count):
    return [pl.BlockSpec(memory_space=pltpu.SMEM)] * count


def prepare_kernel(where, parents, q_ref, do_ref, o_ref, ln_ref, pack_ref, reach_ref, stat):
    def clear(i, carry):
        reach_ref[i] = 0
        return carry

    lax.fori_loop(0, 2 * NBLK, clear, 0)
    for side in range(2):

        def climb(state, side=side):
            block, _ = state
            reach_ref[side * NBLK + block] = 1
            above = parents[block]
            return above, above != block

        lax.while_loop(lambda state: state[1], climb, (where[side], True))

    q = jnp.swapaxes(q_ref[...].astype(F32), 0, 1)
    do = jnp.swapaxes(do_ref[...].astype(F32), 0, 1)
    o = jnp.swapaxes(o_ref[...].astype(F32), 0, 1)
    pack_ref[0:ROWS] = q.reshape(ROWS, HD).astype(BF16)
    pack_ref[ROWS : 2 * ROWS] = do.reshape(ROWS, HD).astype(BF16)
    stat[...] = jnp.zeros_like(stat)
    stat[0, 0:HEADS] = ln_ref[...]
    prod = do * o
    for h in range(HEADS):
        stat[1, h : h + 1] = jnp.sum(prod[h].T, axis=0, keepdims=True)
    for which in range(2):
        rest = stat[which]
        for part in range(3):
            high = rest.astype(BF16)
            start = 2 * ROWS + (which * 3 + part) * STAT_ROWS
            pack_ref[start : start + STAT_ROWS] = high
            rest = rest - high.astype(F32)


def prepare(where, parents, queries, out_grad, outputs, log_norm):
    return pl.pallas_call(
        prepare_kernel,
        out_shape=(
            jax.ShapeDtypeStruct((PACK_ROWS, HD), BF16),
            jax.ShapeDtypeStruct((2 * NBLK,), jnp.int32),
        ),
        in_specs=smem(2) + vmem(4),
        out_specs=(pl.BlockSpec(memory_space=pltpu.VMEM), pl.BlockSpec(memory_space=pltpu.SMEM)),
        scratch_shapes=[pltpu.VMEM((2, STAT_ROWS, BLK), F32)],
        name="prepare",
    )(where, parents, queries, out_grad, outputs, log_norm)


NT = (((1,), (1,)), ((), ()))
NN = (((1,), (0,)), ((), ()))


def mm(a, b, dims):
    return lax.dot_general(a, b, dims, preferred_element_type=F32)


def column_kernel(own, *refs):
    if own:
        where, reach, pack0, pack1, col, part, dq_out, dk, dv, stats = refs
        dq_out[...] = jnp.zeros_like(dq_out)
    else:
        where, reach, pack0, pack1, col, dq_in, part, dq_out, dk, dv, stats = refs
        dq_out[...] = dq_in[...]
    packs = (pack0, pack1)
    for side in range(2):
        for which in range(2):
            base = 2 * ROWS + which * 3 * STAT_ROWS
            total = packs[side][base : base + STAT_ROWS].astype(F32)
            for k in range(1, 3):
                lo = base + k * STAT_ROWS
                total = total + packs[side][lo : lo + STAT_ROWS].astype(F32)
            stats[side, which] = total * LOG2E if which == 0 else total
    first = where[2]

    def per_block(j, carry):
        block = first + 16 * (j // 2) + j % 2
        dk[...] = jnp.zeros_like(dk)
        dv[...] = jnp.zeros_like(dv)
        for side in range(2):

            @pl.when(reach[side * NBLK + block] == 1)
            def _(side=side):
                pack = packs[side]
                keys = col[j, 0:BLK]
                values = col[j, BLK : 2 * BLK]
                keys_t = keys.T
                dk_new = dk[...]
                dv_new = dv[...]
                for c in range(ROWS // CHUNK):
                    lo = c * CHUNK
                    q = pack[lo : lo + CHUNK]
                    do = pack[ROWS + lo : ROWS + lo + CHUNK]
                    norm = jnp.concatenate([stats[side, 0, 2 * c : 2 * c + 1], stats[side, 0, 2 * c + 1 : 2 * c + 2]], 1)
                    dots = jnp.concatenate([stats[side, 1, 2 * c : 2 * c + 1], stats[side, 1, 2 * c + 1 : 2 * c + 2]], 1)
                    probs = jnp.exp2(mm(keys, q, NT) * (SCALING * LOG2E) - norm)
                    if own and side == 0:
                        token = lax.broadcasted_iota(jnp.int32, (BLK, CHUNK), 1) % BLK
                        at = lax.broadcasted_iota(jnp.int32, (BLK, CHUNK), 0)
                        least = jnp.where(block == where[0], 0, -BLK)
                        probs = jnp.where(token - at >= least, probs, 0.0)
                    dprobs = mm(values, do, NT)
                    dscores = (probs * (dprobs - dots) * SCALING).astype(BF16)
                    dv_new = dv_new + mm(probs.astype(BF16), do, NN)
                    dk_new = dk_new + mm(dscores, q, NN)
                    dq_out[side, :, lo : lo + CHUNK] += mm(keys_t, dscores, NN)
                dk[...] = dk_new
                dv[...] = dv_new

        part[j, 0:BLK] = dk[...].astype(part.dtype)
        part[j, BLK : 2 * BLK] = dv[...].astype(part.dtype)
        return carry

    lax.fori_loop(0, 8, per_block, 0)


def column(own, where, reach, pack0, pack1, col, dq=None):
    args = (where, reach, pack0, pack1, col) + (() if own else (dq,))
    return pl.pallas_call(
        functools.partial(column_kernel, own),
        out_shape=(
            jax.ShapeDtypeStruct((8, 2 * BLK, HD), F32 if own else BF16),
            jax.ShapeDtypeStruct((2, HD, ROWS), F32),
        ),
        in_specs=smem(2) + vmem(len(args) - 2),
        out_specs=tuple(vmem(2)),
        scratch_shapes=[
            pltpu.VMEM((BLK, HD), F32),
            pltpu.VMEM((BLK, HD), F32),
            pltpu.VMEM((2, 2, STAT_ROWS, BLK), F32),
        ],
        input_output_aliases={} if own else {5: 1},
        cost_estimate=pl.CostEstimate(flops=600_000_000, bytes_accessed=4_000_000, transcendentals=500_000),
        name="own_column" if own else "column",
    )(*args)


def query_kernel(mine, other, out):
    total = mine[...] + other[...]
    heads = jnp.stack([total[:, h * BLK : (h + 1) * BLK].T for h in range(HEADS)])
    out[...] = jnp.swapaxes(heads, 0, 1).astype(BF16)


def finish_query(mine, other):
    return pl.pallas_call(
        query_kernel,
        out_shape=jax.ShapeDtypeStruct((BLK, HEADS, HD), BF16),
        in_specs=vmem(2),
        out_specs=vmem(1)[0],
        name="finish_query",
    )(mine, other)


def sum_columns_kernel(own, a, b, c, out):
    out[...] = (own[...] + a[...].astype(F32) + b[...].astype(F32) + c[...].astype(F32)).astype(BF16)


def sum_columns(own, a, b, c):
    return pl.pallas_call(
        sum_columns_kernel,
        out_shape=jax.ShapeDtypeStruct((8, 2 * BLK, HD), BF16),
        in_specs=vmem(4),
        out_specs=vmem(1)[0],
        name="sum_columns",
    )(own, a, b, c)


def sum_rows_kernel(parts, out):
    total = parts[0].astype(F32)
    for j in range(1, 8):
        total = total + parts[j].astype(F32)
    low = total.astype(BF16)
    for z in range(KVH):
        out[z] = low


def sum_rows(parts):
    return pl.pallas_call(
        sum_rows_kernel,
        out_shape=jax.ShapeDtypeStruct((KVH, 2 * BLK, HD), BF16),
        in_specs=vmem(1),
        out_specs=vmem(1)[0],
        name="sum_rows",
    )(parts)


def split_heads_kernel(parts, key_out, value_out):
    both = parts[...].astype(F32)
    key_out[...] = jnp.swapaxes(both[:, 0:BLK], 0, 1).astype(BF16)
    value_out[...] = jnp.swapaxes(both[:, BLK : 2 * BLK], 0, 1).astype(BF16)


def split_heads(parts):
    return pl.pallas_call(
        split_heads_kernel,
        out_shape=(jax.ShapeDtypeStruct((BLK, KVH, HD), BF16),) * 2,
        in_specs=vmem(1),
        out_specs=tuple(vmem(2)),
        name="split_heads",
    )(parts)


def body(queries, keys, values, outputs, out_grad, log_norm, parents):
    yh, core, x, yl, z = (lax.axis_index(a) for a in ("yh", "core", "x", "yl", "z"))
    kv = jnp.concatenate(
        [lax.dynamic_index_in_dim(keys, z, 1, False), lax.dynamic_index_in_dim(values, z, 1, False)], 0
    )
    base = 16 * yh + 2 * x + yl
    ours, theirs = base + 8 * core, base + 8 * (1 - core)

    def where(distance):
        return jnp.stack([ours, theirs, 8 * core + 2 * ((x + distance) % 4)]).astype(jnp.int32)

    pack0, reach = prepare(where(0), parents, queries, out_grad, outputs, log_norm)
    pack1 = shift(pack0, "core", 1)
    col = lax.all_to_all(jnp.broadcast_to(kv[None], (8, 2 * BLK, HD)), Y, 0, 0)
    col_back, col_next, col_far = shift(col, "x", 1), shift(col, "x", -1), shift(col, "x", 2)
    part_own, dq = column(True, where(0), reach, pack0, pack1, col)
    part_back, dq = column(False, where(-1), reach, pack0, pack1, col_back, dq)
    got_back = shift(part_back, "x", -1)
    part_next, dq = column(False, where(1), reach, pack0, pack1, col_next, dq)
    got_next = shift(part_next, "x", 1)
    part_far, dq = column(False, where(2), reach, pack0, pack1, col_far, dq)
    got_far = shift(part_far, "x", 2)
    dq_other = shift(dq[1], "core", 1)
    query_grad = finish_query(dq[0], dq_other)
    row = lax.all_to_all(sum_columns(part_own, got_back, got_next, got_far), Y, 0, 0)
    heads = lax.all_to_all(sum_rows(row), "z", 0, 0)
    key_grad, value_grad = split_heads(heads)
    return query_grad, key_grad, value_grad


def solution(mesh):
    fine = Mesh(mesh.devices.reshape(4, 2, 4, 2, 8), ("yh", "core", "x", "yl", "z"))
    tokens = ("yh", "core", "x", "yl")
    in_specs = (
        P(tokens, "z", None),
        P(tokens, None, None),
        P(tokens, None, None),
        P(tokens, "z", None),
        P(tokens, "z", None),
        P("z", tokens),
        P(),
    )
    out_specs = (P(tokens, "z", None), P(tokens, None, None), P(tokens, None, None))
    return jax.shard_map(body, mesh=fine, in_specs=in_specs, out_specs=out_specs, check_vma=False)
```

```python
import functools

import jax
import jax.numpy as jnp
from jax import lax
from jax.experimental import pallas as pl
from jax.experimental.pallas import tpu as pltpu
from jax.sharding import Mesh, PartitionSpec as P

BLK = 128
HD = 128
HEADS = 6
ROWS = HEADS * BLK
NBLK = 64
KVH = 8
SIDES = 8
DISTANCES = (0, 1, -1, 2)
Y = ("yh", "yl")
STAT_ROWS = 16
PACK_ROWS = 2 * ROWS + 6 * STAT_ROWS
SCALING = HD ** -0.5
LOG2E = 1.4426950408889634
CHUNK = 2 * BLK
F32 = jnp.float32
BF16 = jnp.bfloat16


def shift(block, axis, distance):
    size = lax.axis_size(axis)
    return lax.ppermute(block, axis, [(i, (i + distance) % size) for i in range(size)])


def vmem(count):
    return [pl.BlockSpec(memory_space=pltpu.VMEM)] * count


def smem(count):
    return [pl.BlockSpec(memory_space=pltpu.SMEM)] * count


def prepare_kernel(ids, parents, q_ref, do_ref, o_ref, ln_ref, pack_ref, reach_ref, stat):
    def clear(i, carry):
        reach_ref[i] = 0
        return carry

    lax.fori_loop(0, SIDES * NBLK, clear, 0)

    def walk(side, carry):
        def climb(state):
            block, _ = state
            reach_ref[side * NBLK + block] = 1
            above = parents[block]
            return above, above != block

        lax.while_loop(lambda state: state[1], climb, (ids[side], True))
        return carry

    lax.fori_loop(0, SIDES, walk, 0)

    pack_ref[0:ROWS] = q_ref[...].reshape(ROWS, HD)
    pack_ref[ROWS : 2 * ROWS] = do_ref[...].reshape(ROWS, HD)
    stat[...] = jnp.zeros_like(stat)
    stat[0, 0:HEADS] = ln_ref[...]
    for h in range(HEADS):
        prod = do_ref[h].astype(F32) * o_ref[h].astype(F32)
        stat[1, h : h + 1] = jnp.sum(prod.T, axis=0, keepdims=True)
    for which in range(2):
        rest = stat[which]
        for part in range(3):
            high = rest.astype(BF16)
            start = 2 * ROWS + (which * 3 + part) * STAT_ROWS
            pack_ref[start : start + STAT_ROWS] = high
            rest = rest - high.astype(F32)


def prepare(ids, parents, queries, out_grad, outputs, log_norm):
    return pl.pallas_call(
        prepare_kernel,
        out_shape=(
            jax.ShapeDtypeStruct((PACK_ROWS, HD), BF16),
            jax.ShapeDtypeStruct((SIDES * NBLK,), jnp.int32),
        ),
        in_specs=smem(2) + vmem(4),
        out_specs=(pl.BlockSpec(memory_space=pltpu.VMEM), pl.BlockSpec(memory_space=pltpu.SMEM)),
        scratch_shapes=[pltpu.VMEM((2, STAT_ROWS, BLK), F32)],
        cost_estimate=pl.CostEstimate(flops=4_000_000, bytes_accessed=1_000_000, transcendentals=0),
        name="prepare",
    )(ids, parents, queries, out_grad, outputs, log_norm)


NT = (((1,), (1,)), ((), ()))
NN = (((1,), (0,)), ((), ()))


def mm(a, b, dims):
    return lax.dot_general(a, b, dims, preferred_element_type=F32)


def attend_kernel(ids, reach, *refs):
    packs, (col, part), grads, (dk, dv, stats) = refs[:8], refs[8:10], refs[10:18], refs[18:]
    for side in range(SIDES):
        grads[side][...] = jnp.zeros((HD, ROWS), F32)
        for which in range(2):
            base = 2 * ROWS + which * 3 * STAT_ROWS
            total = packs[side][base : base + STAT_ROWS].astype(F32)
            for k in range(1, 3):
                lo = base + k * STAT_ROWS
                total = total + packs[side][lo : lo + STAT_ROWS].astype(F32)
            stats[side, which] = total * LOG2E if which == 0 else total
    first = ids[SIDES]

    def per_block(j, carry):
        block = first + 16 * (j // 2) + j % 2
        dk[...] = jnp.zeros_like(dk)
        dv[...] = jnp.zeros_like(dv)
        for side in range(SIDES):

            @pl.when(reach[side * NBLK + block] == 1)
            def _(side=side):
                pack = packs[side]
                keys = col[j, 0:BLK]
                values = col[j, BLK : 2 * BLK]
                keys_t = keys.T
                dk_new = dk[...]
                dv_new = dv[...]
                for c in range(ROWS // CHUNK):
                    lo = c * CHUNK
                    q = pack[lo : lo + CHUNK]
                    do = pack[ROWS + lo : ROWS + lo + CHUNK]
                    norm, dots = (
                        jnp.concatenate(
                            [stats[side, which, 2 * c : 2 * c + 1], stats[side, which, 2 * c + 1 : 2 * c + 2]], 1
                        )
                        for which in range(2)
                    )
                    probs = jnp.exp2(mm(keys, q, NT) * (SCALING * LOG2E) - norm)
                    if side == 0:
                        token = lax.broadcasted_iota(jnp.int32, (BLK, CHUNK), 1) % BLK
                        at = lax.broadcasted_iota(jnp.int32, (BLK, CHUNK), 0)
                        least = jnp.where(block == ids[0], 0, -BLK)
                        probs = jnp.where(token - at >= least, probs, 0.0)
                    dprobs = mm(values, do, NT)
                    dscores = (probs * (dprobs - dots) * SCALING).astype(BF16)
                    dv_new = dv_new + mm(probs.astype(BF16), do, NN)
                    dk_new = dk_new + mm(dscores, q, NN)
                    grads[side][:, lo : lo + CHUNK] += mm(keys_t, dscores, NN)
                dk[...] = dk_new
                dv[...] = dv_new

        part[j, 0:BLK] = dk[...].astype(BF16)
        part[j, BLK : 2 * BLK] = dv[...].astype(BF16)
        return carry

    lax.fori_loop(0, 8, per_block, 0)


def attend(ids, reach, packs, col):
    return pl.pallas_call(
        attend_kernel,
        out_shape=(jax.ShapeDtypeStruct((8, 2 * BLK, HD), BF16),)
        + (jax.ShapeDtypeStruct((HD, ROWS), F32),) * SIDES,
        in_specs=smem(2) + vmem(SIDES + 1),
        out_specs=tuple(vmem(SIDES + 1)),
        scratch_shapes=[
            pltpu.VMEM((BLK, HD), F32),
            pltpu.VMEM((BLK, HD), F32),
            pltpu.VMEM((SIDES, 2, STAT_ROWS, BLK), F32),
        ],
        compiler_params=pltpu.CompilerParams(vmem_limit_bytes=32 * 1024 * 1024),
        cost_estimate=pl.CostEstimate(flops=2_000_000_000, bytes_accessed=8_000_000, transcendentals=2_000_000),
        name="attend",
    )(ids, reach, *packs, col)


def add_cores_kernel(*refs):
    for a, b, out in zip(refs[0:4], refs[4:8], refs[8:12], strict=True):
        out[...] = a[...] + b[...]


def add_cores(mine, other):
    return pl.pallas_call(
        add_cores_kernel,
        out_shape=(jax.ShapeDtypeStruct((HD, ROWS), F32),) * 4,
        in_specs=vmem(8),
        out_specs=tuple(vmem(4)),
        cost_estimate=pl.CostEstimate(flops=400_000, bytes_accessed=5_000_000, transcendentals=0),
        name="add_cores",
    )(*mine, *other)


def query_kernel(a, b, c, d, out):
    total = (a[...] + b[...]) + (c[...] + d[...])
    for h in range(HEADS):
        out[h] = total[:, h * BLK : (h + 1) * BLK].T.astype(BF16)


def finish_query(parts):
    return pl.pallas_call(
        query_kernel,
        out_shape=jax.ShapeDtypeStruct((HEADS, BLK, HD), BF16),
        in_specs=vmem(4),
        out_specs=vmem(1)[0],
        cost_estimate=pl.CostEstimate(flops=400_000, bytes_accessed=2_000_000, transcendentals=0),
        name="finish_query",
    )(*parts)


def sum_rows_kernel(parts, out):
    total = parts[0].astype(F32)
    for j in range(1, 8):
        total = total + parts[j].astype(F32)
    low = total.astype(BF16)
    for z in range(KVH):
        out[z] = low


def sum_rows(parts):
    return pl.pallas_call(
        sum_rows_kernel,
        out_shape=jax.ShapeDtypeStruct((KVH, 2 * BLK, HD), BF16),
        in_specs=vmem(1),
        out_specs=vmem(1)[0],
        name="sum_rows",
    )(parts)


def split_heads_kernel(parts, key_out, value_out):
    both = parts[...].astype(F32)
    key_out[...] = jnp.swapaxes(both[:, 0:BLK], 0, 1).astype(BF16)
    value_out[...] = jnp.swapaxes(both[:, BLK : 2 * BLK], 0, 1).astype(BF16)


def split_heads(parts):
    return pl.pallas_call(
        split_heads_kernel,
        out_shape=(jax.ShapeDtypeStruct((BLK, KVH, HD), BF16),) * 2,
        in_specs=vmem(1),
        out_specs=tuple(vmem(2)),
        name="split_heads",
    )(parts)


def body(queries, keys, values, outputs, out_grad, log_norm, parents):
    yh, core, x, yl, z = (lax.axis_index(a) for a in ("yh", "core", "x", "yl", "z"))
    kv = jnp.concatenate(
        [lax.dynamic_index_in_dim(keys, z, 1, False), lax.dynamic_index_in_dim(values, z, 1, False)], 0
    )
    ids = [
        16 * yh + 8 * (core if side < 4 else 1 - core) + 2 * ((x + DISTANCES[side % 4]) % 4) + yl
        for side in range(SIDES)
    ]
    ids = jnp.stack([*ids, 8 * core + 2 * x]).astype(jnp.int32)

    col = lax.all_to_all(jnp.broadcast_to(kv[None], (8, 2 * BLK, HD)), Y, 0, 0)
    queries, out_grad, outputs = (jnp.swapaxes(a, 0, 1) for a in (queries, out_grad, outputs))
    pack, reach = prepare(ids, parents, queries, out_grad, outputs, log_norm)
    packs = [pack] + [shift(pack, "x", -d) for d in DISTANCES[1:]]
    packs = packs + [shift(p, "core", 1) for p in packs]
    part, *grads = attend(ids, reach, packs, col)
    row = lax.all_to_all(part, Y, 0, 0)
    sums = add_cores(grads[:4], [shift(g, "core", 1) for g in grads[4:]])
    query_grad = finish_query([sums[0]] + [shift(g, "x", d) for g, d in zip(sums[1:], DISTANCES[1:], strict=True)])
    heads = lax.all_to_all(sum_rows(row), "z", 0, 0)
    key_grad, value_grad = split_heads(heads)
    return jnp.swapaxes(query_grad, 0, 1), key_grad, value_grad


def solution(mesh):
    fine = Mesh(mesh.devices.reshape(4, 2, 4, 2, 8), ("yh", "core", "x", "yl", "z"))
    tokens = ("yh", "core", "x", "yl")
    in_specs = (
        P(tokens, "z", None),
        P(tokens, None, None),
        P(tokens, None, None),
        P(tokens, "z", None),
        P(tokens, "z", None),
        P("z", tokens),
        P(),
    )
    out_specs = (P(tokens, "z", None), P(tokens, None, None), P(tokens, None, None))
    return jax.shard_map(body, mesh=fine, in_specs=in_specs, out_specs=out_specs, check_vma=False)
```

```python
import functools

import jax
import jax.numpy as jnp
from jax import lax
from jax.experimental import pallas as pl
from jax.experimental.pallas import tpu as pltpu
from jax.sharding import Mesh, PartitionSpec as P

BLK = 128
HD = 128
HEADS = 6
ROWS = HEADS * BLK
NBLK = 64
KVH = 8
SIDES = 8
DISTANCES = (0, 1, -1, 2)
Y = ("yh", "yl")
STAT_ROWS = 16
PACK_ROWS = 2 * ROWS + 3 * STAT_ROWS
DOTS = 8
SCALING = HD ** -0.5
LOG2E = 1.4426950408889634
PER_STEP = 2
F32 = jnp.float32
BF16 = jnp.bfloat16


def shift(block, axis, distance):
    size = lax.axis_size(axis)
    return lax.ppermute(block, axis, [(i, (i + distance) % size) for i in range(size)])


def room(mebibytes):
    return pltpu.CompilerParams(vmem_limit_bytes=mebibytes * 1024 * 1024)


def vmem(count):
    return [pl.BlockSpec(memory_space=pltpu.VMEM)] * count


def anywhere(count):
    return [pl.BlockSpec(memory_space=pl.ANY)] * count


def smem(count):
    return [pl.BlockSpec(memory_space=pltpu.SMEM)] * count


def reach_kernel(ids, parents, pairs, low, high):
    def step(block, carry):
        above = parents[block]
        root = above == block
        bit = jnp.left_shift(jnp.int32(1), block % 32)
        low[block] = jnp.where(root, 0, low[above]) | jnp.where(block < 32, bit, 0)
        high[block] = jnp.where(root, 0, high[above]) | jnp.where(block < 32, 0, bit)
        return carry

    lax.fori_loop(0, NBLK, step, 0)
    first = ids[SIDES]

    def look(k, count):
        side, j = k // 8, k % 8
        block = first + 16 * (j // 2) + j % 2
        mine = ids[side]
        word = jnp.where(block < 32, low[mine], high[mine])
        take = ((jnp.right_shift(word, block % 32) & 1) == 1) & (block != mine)
        pairs[1 + count] = k
        return count + take.astype(jnp.int32)

    count = lax.fori_loop(0, SIDES * 8, look, 0)
    pairs[0] = count
    pairs[1 + count] = 0


def reach(ids, parents):
    return pl.pallas_call(
        reach_kernel,
        out_shape=jax.ShapeDtypeStruct((SIDES * 8 + 2,), jnp.int32),
        in_specs=smem(2),
        out_specs=smem(1)[0],
        scratch_shapes=[pltpu.SMEM((NBLK,), jnp.int32)] * 2,
        cost_estimate=pl.CostEstimate(flops=1000, bytes_accessed=1000, transcendentals=0),
        compiler_params=room(1),
        name="reach",
    )(ids, parents)


def prepare_kernel(q_hbm, do_hbm, o_hbm, ln_hbm, pack_ref, q_ref, do_ref, o_ref, ln_ref, stat, sems):
    routes = ((do_hbm, do_ref), (o_hbm, o_ref), (ln_hbm, ln_ref), (q_hbm, q_ref))
    copies = [pltpu.make_async_copy(src, dst, sems.at[i]) for i, (src, dst) in enumerate(routes)]
    for copy in copies:
        copy.start()
    stat[...] = jnp.zeros_like(stat)
    for copy in copies:
        copy.wait()
    pack_ref[0:ROWS] = q_ref[...].reshape(ROWS, HD)
    pack_ref[ROWS : 2 * ROWS] = do_ref[...].reshape(ROWS, HD)
    stat[0:HEADS] = ln_ref[...]
    for h in range(HEADS):
        prod = do_ref[h].astype(F32) * o_ref[h].astype(F32)
        stat[DOTS + h : DOTS + h + 1] = jnp.sum(prod.T, axis=0, keepdims=True)
    rest = stat[...]
    for part in range(3):
        high = rest.astype(BF16)
        start = 2 * ROWS + part * STAT_ROWS
        pack_ref[start : start + STAT_ROWS] = high
        rest = rest - high.astype(F32)


def prepare(queries, out_grad, outputs, log_norm):
    return pl.pallas_call(
        prepare_kernel,
        out_shape=jax.ShapeDtypeStruct((PACK_ROWS, HD), BF16),
        in_specs=anywhere(4),
        out_specs=vmem(1)[0],
        scratch_shapes=[pltpu.VMEM((HEADS, BLK, HD), BF16)] * 3
        + [pltpu.VMEM((HEADS, BLK), F32), pltpu.VMEM((STAT_ROWS, BLK), F32), pltpu.SemaphoreType.DMA((4,))],
        cost_estimate=pl.CostEstimate(flops=4_000_000, bytes_accessed=1_000_000, transcendentals=0),
        compiler_params=room(60),
        name="prepare",
    )(queries, out_grad, outputs, log_norm)


NT = (((1,), (1,)), ((), ()))
NN = (((1,), (0,)), ((), ()))


def mm(a, b, dims):
    return lax.dot_general(a, b, dims, preferred_element_type=F32)


def attend_kernel(ids, pairs, *refs):
    remote, (col_hbm, part, mine, other, packs, col, sums, low, both, sems, outs) = refs[:8], refs[8:]
    copies = [pltpu.make_async_copy(remote[side], packs.at[side], sems.at[side]) for side in range(SIDES)]
    copies.append(pltpu.make_async_copy(col_hbm, col, sems.at[SIDES]))
    copies[SIDES].start()
    for copy in copies[:SIDES]:
        copy.start()
    sums[...] = jnp.zeros_like(sums)
    both[...] = jnp.zeros_like(both)

    def visit(work, diagonal=False):
        rows = [
            packs[side, 2 * ROWS : 2 * ROWS + STAT_ROWS].astype(F32)
            + packs[side, 2 * ROWS + STAT_ROWS : 2 * ROWS + 2 * STAT_ROWS].astype(F32)
            + packs[side, 2 * ROWS + 2 * STAT_ROWS : PACK_ROWS].astype(F32)
            for side, _, _ in work
        ]
        norms = [jnp.concatenate([r[h : h + 1] for h in range(HEADS)], 1) * LOG2E for r in rows]
        dots = [jnp.concatenate([r[DOTS + h : DOTS + h + 1] for h in range(HEADS)], 1) for r in rows]
        probs = [
            jnp.exp2(mm(col[j, 0:BLK], packs[side, 0:ROWS], NT) * (SCALING * LOG2E) - norm)
            for (side, j, _), norm in zip(work, norms, strict=True)
        ]
        dprobs = [mm(col[j, BLK : 2 * BLK], packs[side, ROWS : 2 * ROWS], NT) for side, j, _ in work]
        if diagonal:
            token = lax.broadcasted_iota(jnp.int32, (BLK, ROWS), 1) % BLK
            place = lax.broadcasted_iota(jnp.int32, (BLK, ROWS), 0)
            probs = [jnp.where(token >= place, p, 0.0) for p in probs]
        probs = [p if use is None else jnp.where(use, p, 0.0) for p, (_, _, use) in zip(probs, work, strict=True)]
        dscores = [(p * (d - dot) * SCALING).astype(BF16) for p, d, dot in zip(probs, dprobs, dots, strict=True)]
        dv = [mm(p.astype(BF16), packs[side, ROWS : 2 * ROWS], NN) for p, (side, _, _) in zip(probs, work, strict=True)]
        dk = [mm(d, packs[side, 0:ROWS], NN) for d, (side, _, _) in zip(dscores, work, strict=True)]
        dq = [mm(col[j, 0:BLK].T, d, NN) for d, (_, j, _) in zip(dscores, work, strict=True)]
        for (side, j, _), k_part, v_part, q_part in zip(work, dk, dv, dq, strict=True):
            sums[j, 0:BLK] += k_part
            sums[j, BLK : 2 * BLK] += v_part
            both[side] += q_part

    own = ids[0]
    copies[SIDES].wait()
    copies[0].wait()
    visit([(0, 2 * (own // 16) + own % 2, None)], diagonal=True)
    for copy in copies[1:SIDES]:
        copy.wait()

    def step(i, carry):
        work = []
        for k in range(PER_STEP):
            at = PER_STEP * i + k
            code = pairs[1 + jnp.minimum(at, SIDES * 8)]
            work.append((code // 8, code % 8, (at < pairs[0]) if k else None))
        visit(work)
        return carry

    lax.fori_loop(0, (pairs[0] + PER_STEP - 1) // PER_STEP, step, 0)
    low[...] = sums[...].astype(BF16)
    copies = [
        pltpu.make_async_copy(low, part, outs.at[0]),
        pltpu.make_async_copy(both.at[4:8], other, outs.at[1]),
        pltpu.make_async_copy(both.at[0:4], mine, outs.at[2]),
    ]
    for copy in copies:
        copy.start()
    for copy in copies:
        copy.wait()


def attend(ids, pairs, packs, col):
    return pl.pallas_call(
        attend_kernel,
        out_shape=(
            jax.ShapeDtypeStruct((8, 2 * BLK, HD), BF16),
            jax.ShapeDtypeStruct((4, HD, ROWS), F32),
            jax.ShapeDtypeStruct((4, HD, ROWS), F32),
        ),
        in_specs=smem(2) + anywhere(SIDES + 1),
        out_specs=tuple(anywhere(3)),
        scratch_shapes=[
            pltpu.VMEM((SIDES, PACK_ROWS, HD), BF16),
            pltpu.VMEM((8, 2 * BLK, HD), BF16),
            pltpu.VMEM((8, 2 * BLK, HD), F32),
            pltpu.VMEM((8, 2 * BLK, HD), BF16),
            pltpu.VMEM((SIDES, HD, ROWS), F32),
            pltpu.SemaphoreType.DMA((SIDES + 1,)),
            pltpu.SemaphoreType.DMA((3,)),
        ],
        compiler_params=room(56),
        cost_estimate=pl.CostEstimate(flops=2_000_000_000, bytes_accessed=8_000_000, transcendentals=2_000_000),
        name="attend",
    )(ids, pairs, *packs, col)


def add_cores_kernel(mine, other, keep, *sends):
    keep[...] = mine[0] + other[0]
    for i, send in enumerate(sends):
        send[...] = (mine[i + 1] + other[i + 1]).astype(BF16)


def add_cores(mine, other):
    return pl.pallas_call(
        add_cores_kernel,
        out_shape=(jax.ShapeDtypeStruct((HD, ROWS), F32),) + (jax.ShapeDtypeStruct((HD, ROWS), BF16),) * 3,
        in_specs=vmem(2),
        out_specs=tuple(vmem(4)),
        cost_estimate=pl.CostEstimate(flops=400_000, bytes_accessed=5_000_000, transcendentals=0),
        compiler_params=room(8),
        name="add_cores",
    )(mine, other)


def query_kernel(a, b, c, d, out):
    total = (a[...] + b[...].astype(F32)) + (c[...].astype(F32) + d[...].astype(F32))
    for h in range(HEADS):
        out[h] = total[:, h * BLK : (h + 1) * BLK].T.astype(BF16)


def finish_query(parts):
    return pl.pallas_call(
        query_kernel,
        out_shape=jax.ShapeDtypeStruct((HEADS, BLK, HD), BF16),
        in_specs=vmem(4),
        out_specs=vmem(1)[0],
        cost_estimate=pl.CostEstimate(flops=400_000, bytes_accessed=2_000_000, transcendentals=0),
        compiler_params=room(4),
        name="finish_query",
    )(*parts)


def sum_rows_kernel(parts, out):
    total = parts[0].astype(F32)
    for j in range(1, 8):
        total = total + parts[j].astype(F32)
    low = total.astype(BF16)
    for z in range(KVH):
        out[z] = low


def sum_rows(parts):
    return pl.pallas_call(
        sum_rows_kernel,
        out_shape=jax.ShapeDtypeStruct((KVH, 2 * BLK, HD), BF16),
        in_specs=vmem(1),
        out_specs=vmem(1)[0],
        compiler_params=room(4),
        name="sum_rows",
    )(parts)


def split_heads_kernel(parts, key_out, value_out):
    both = parts[...].astype(F32)
    key_out[...] = jnp.swapaxes(both[:, 0:BLK], 0, 1).astype(BF16)
    value_out[...] = jnp.swapaxes(both[:, BLK : 2 * BLK], 0, 1).astype(BF16)


def split_heads(parts):
    return pl.pallas_call(
        split_heads_kernel,
        out_shape=(jax.ShapeDtypeStruct((BLK, KVH, HD), BF16),) * 2,
        in_specs=vmem(1),
        out_specs=tuple(vmem(2)),
        compiler_params=room(4),
        name="split_heads",
    )(parts)


def body(queries, keys, values, outputs, out_grad, log_norm, parents):
    yh, core, x, yl, z = (lax.axis_index(a) for a in ("yh", "core", "x", "yl", "z"))
    kv = jnp.concatenate(
        [lax.dynamic_index_in_dim(keys, z, 1, False), lax.dynamic_index_in_dim(values, z, 1, False)], 0
    )
    ids = [
        16 * yh + 8 * (core if side < 4 else 1 - core) + 2 * ((x + DISTANCES[side % 4]) % 4) + yl
        for side in range(SIDES)
    ]
    ids = jnp.stack([*ids, 8 * core + 2 * x]).astype(jnp.int32)

    queries, out_grad, outputs = (jnp.swapaxes(a, 0, 1) for a in (queries, out_grad, outputs))
    pack = prepare(queries, out_grad, outputs, log_norm)
    pack, kv = lax.optimization_barrier((pack, kv))
    near = [shift(pack, "x", -d) for d in DISTANCES[1:]]
    col = lax.all_to_all(jnp.broadcast_to(kv[None], (8, 2 * BLK, HD)), Y, 0, 0)
    pairs = reach(ids, parents)
    swapped = [shift(pack, "core", 1)]
    pairs, ids, near[0] = lax.optimization_barrier((pairs, ids, near[0]))
    swapped += [shift(p, "core", 1) for p in near]
    packs = [pack, *near, *swapped]
    part, mine, other = attend(ids, pairs, packs, col)
    row = lax.all_to_all(part, Y, 0, 0)
    keep, *sends = add_cores(mine, shift(other, "core", 1))
    got = [shift(g, "x", d) for g, d in zip(sends, DISTANCES[1:], strict=True)]
    row, keep, *got = lax.optimization_barrier((row, keep, *got))
    heads = lax.all_to_all(sum_rows(row), "z", 0, 0)
    query_grad = finish_query([keep, *got])
    key_grad, value_grad = split_heads(heads)
    return jnp.swapaxes(query_grad, 0, 1), key_grad, value_grad


def solution(mesh):
    fine = Mesh(mesh.devices.reshape(4, 2, 4, 2, 8), ("yh", "core", "x", "yl", "z"))
    tokens = ("yh", "core", "x", "yl")
    in_specs = (
        P(tokens, "z", None),
        P(tokens, None, None),
        P(tokens, None, None),
        P(tokens, "z", None),
        P(tokens, "z", None),
        P("z", tokens),
        P(),
    )
    out_specs = (P(tokens, "z", None), P(tokens, None, None), P(tokens, None, None))
    return jax.shard_map(body, mesh=fine, in_specs=in_specs, out_specs=out_specs, check_vma=False)
```

```python
import functools

import jax
import jax.numpy as jnp
from jax import lax
from jax.experimental import pallas as pl
from jax.experimental.pallas import tpu as pltpu
from jax.sharding import Mesh, PartitionSpec as P

BLK = 128
HD = 128
HEADS = 6
ROWS = HEADS * BLK
NBLK = 64
KVH = 8
SIDES = 8
DISTANCES = (0, 1, -1, 2)
Y = ("yh", "yl")
STAT_ROWS = 16
PACK_ROWS = 2 * ROWS + 3 * STAT_ROWS
DOTS = 8
SCALING = HD ** -0.5
LOG2E = 1.4426950408889634
PER_STEP = 2
F32 = jnp.float32
BF16 = jnp.bfloat16


def shift(block, axis, distance):
    size = lax.axis_size(axis)
    return lax.ppermute(block, axis, [(i, (i + distance) % size) for i in range(size)])


def room(mebibytes):
    return pltpu.CompilerParams(vmem_limit_bytes=mebibytes * 1024 * 1024)


def vmem(count):
    return [pl.BlockSpec(memory_space=pltpu.VMEM)] * count


def anywhere(count):
    return [pl.BlockSpec(memory_space=pl.ANY)] * count


def smem(count):
    return [pl.BlockSpec(memory_space=pltpu.SMEM)] * count


def reach_kernel(ids, parents, pairs, low, high):
    def step(block, carry):
        above = parents[block]
        root = above == block
        bit = jnp.left_shift(jnp.int32(1), block % 32)
        low[block] = jnp.where(root, 0, low[above]) | jnp.where(block < 32, bit, 0)
        high[block] = jnp.where(root, 0, high[above]) | jnp.where(block < 32, 0, bit)
        return carry

    lax.fori_loop(0, NBLK, step, 0)
    first = ids[SIDES]

    def look(k, count):
        side, j = k // 8, k % 8
        block = first + 16 * (j // 2) + j % 2
        mine = ids[side]
        word = jnp.where(block < 32, low[mine], high[mine])
        take = ((jnp.right_shift(word, block % 32) & 1) == 1) & (block != mine)
        pairs[1 + count] = k
        return count + take.astype(jnp.int32)

    count = lax.fori_loop(0, SIDES * 8, look, 0)
    pairs[0] = count
    pairs[1 + count] = 0


def reach(ids, parents):
    return pl.pallas_call(
        reach_kernel,
        out_shape=jax.ShapeDtypeStruct((SIDES * 8 + 2,), jnp.int32),
        in_specs=smem(2),
        out_specs=smem(1)[0],
        scratch_shapes=[pltpu.SMEM((NBLK,), jnp.int32)] * 2,
        cost_estimate=pl.CostEstimate(flops=60_000_000_000, bytes_accessed=1000, transcendentals=0),
        compiler_params=room(1),
        name="reach",
    )(ids, parents)


def prepare_kernel(q_hbm, do_hbm, o_hbm, ln_hbm, pack_ref, q_ref, do_ref, o_ref, ln_ref, stat, sems):
    routes = ((do_hbm, do_ref), (o_hbm, o_ref), (ln_hbm, ln_ref), (q_hbm, q_ref))
    copies = [pltpu.make_async_copy(src, dst, sems.at[i]) for i, (src, dst) in enumerate(routes)]
    for copy in copies:
        copy.start()
    stat[...] = jnp.zeros_like(stat)
    for copy in copies:
        copy.wait()
    pack_ref[0:ROWS] = q_ref[...].reshape(ROWS, HD)
    pack_ref[ROWS : 2 * ROWS] = do_ref[...].reshape(ROWS, HD)
    stat[0:HEADS] = ln_ref[...]
    for h in range(HEADS):
        prod = do_ref[h].astype(F32) * o_ref[h].astype(F32)
        stat[DOTS + h : DOTS + h + 1] = jnp.sum(prod.T, axis=0, keepdims=True)
    rest = stat[...]
    for part in range(3):
        high = rest.astype(BF16)
        start = 2 * ROWS + part * STAT_ROWS
        pack_ref[start : start + STAT_ROWS] = high
        rest = rest - high.astype(F32)


def prepare(queries, out_grad, outputs, log_norm):
    return pl.pallas_call(
        prepare_kernel,
        out_shape=jax.ShapeDtypeStruct((PACK_ROWS, HD), BF16),
        in_specs=anywhere(4),
        out_specs=vmem(1)[0],
        scratch_shapes=[pltpu.VMEM((HEADS, BLK, HD), BF16)] * 3
        + [pltpu.VMEM((HEADS, BLK), F32), pltpu.VMEM((STAT_ROWS, BLK), F32), pltpu.SemaphoreType.DMA((4,))],
        cost_estimate=pl.CostEstimate(flops=4_000_000, bytes_accessed=1_000_000, transcendentals=0),
        compiler_params=room(60),
        name="prepare",
    )(queries, out_grad, outputs, log_norm)


NT = (((1,), (1,)), ((), ()))
NN = (((1,), (0,)), ((), ()))


def mm(a, b, dims):
    return lax.dot_general(a, b, dims, preferred_element_type=F32)


def attend_kernel(ids, pairs, *refs):
    remote, (col_hbm, part, mine, other, packs, col, sums, low, both, sems, outs) = refs[:8], refs[8:]
    copies = [pltpu.make_async_copy(remote[side], packs.at[side], sems.at[side]) for side in range(SIDES)]
    copies.append(pltpu.make_async_copy(col_hbm, col, sems.at[SIDES]))
    copies[SIDES].start()
    for copy in copies[:SIDES]:
        copy.start()
    sums[...] = jnp.zeros_like(sums)
    both[...] = jnp.zeros_like(both)

    def visit(work, diagonal=False):
        rows = [
            packs[side, 2 * ROWS : 2 * ROWS + STAT_ROWS].astype(F32)
            + packs[side, 2 * ROWS + STAT_ROWS : 2 * ROWS + 2 * STAT_ROWS].astype(F32)
            + packs[side, 2 * ROWS + 2 * STAT_ROWS : PACK_ROWS].astype(F32)
            for side, _, _ in work
        ]
        norms = [jnp.concatenate([r[h : h + 1] for h in range(HEADS)], 1) * LOG2E for r in rows]
        dots = [jnp.concatenate([r[DOTS + h : DOTS + h + 1] for h in range(HEADS)], 1) for r in rows]
        probs = [
            jnp.exp2(mm(col[j, 0:BLK], packs[side, 0:ROWS], NT) * (SCALING * LOG2E) - norm)
            for (side, j, _), norm in zip(work, norms, strict=True)
        ]
        dprobs = [mm(col[j, BLK : 2 * BLK], packs[side, ROWS : 2 * ROWS], NT) for side, j, _ in work]
        if diagonal:
            token = lax.broadcasted_iota(jnp.int32, (BLK, ROWS), 1) % BLK
            place = lax.broadcasted_iota(jnp.int32, (BLK, ROWS), 0)
            probs = [jnp.where(token >= place, p, 0.0) for p in probs]
        probs = [p if use is None else jnp.where(use, p, 0.0) for p, (_, _, use) in zip(probs, work, strict=True)]
        dscores = [(p * (d - dot) * SCALING).astype(BF16) for p, d, dot in zip(probs, dprobs, dots, strict=True)]
        dv = [mm(p.astype(BF16), packs[side, ROWS : 2 * ROWS], NN) for p, (side, _, _) in zip(probs, work, strict=True)]
        dk = [mm(d, packs[side, 0:ROWS], NN) for d, (side, _, _) in zip(dscores, work, strict=True)]
        dq = [mm(col[j, 0:BLK].T, d, NN) for d, (_, j, _) in zip(dscores, work, strict=True)]
        for (side, j, _), k_part, v_part, q_part in zip(work, dk, dv, dq, strict=True):
            sums[j, 0:BLK] += k_part
            sums[j, BLK : 2 * BLK] += v_part
            both[side] += q_part

    own = ids[0]
    copies[SIDES].wait()
    copies[0].wait()
    visit([(0, 2 * (own // 16) + own % 2, None)], diagonal=True)
    for copy in copies[1:SIDES]:
        copy.wait()

    def step(i, carry):
        work = []
        for k in range(PER_STEP):
            at = PER_STEP * i + k
            code = pairs[1 + jnp.minimum(at, SIDES * 8)]
            work.append((code // 8, code % 8, (at < pairs[0]) if k else None))
        visit(work)
        return carry

    lax.fori_loop(0, (pairs[0] + PER_STEP - 1) // PER_STEP, step, 0)
    low[...] = sums[...].astype(BF16)
    copies = [
        pltpu.make_async_copy(low, part, outs.at[0]),
        pltpu.make_async_copy(both.at[4:8], other, outs.at[1]),
        pltpu.make_async_copy(both.at[0:4], mine, outs.at[2]),
    ]
    for copy in copies:
        copy.start()
    for copy in copies:
        copy.wait()


def attend(ids, pairs, packs, col):
    return pl.pallas_call(
        attend_kernel,
        out_shape=(
            jax.ShapeDtypeStruct((8, 2 * BLK, HD), BF16),
            jax.ShapeDtypeStruct((4, HD, ROWS), F32),
            jax.ShapeDtypeStruct((4, HD, ROWS), F32),
        ),
        in_specs=smem(2) + anywhere(SIDES + 1),
        out_specs=tuple(anywhere(3)),
        scratch_shapes=[
            pltpu.VMEM((SIDES, PACK_ROWS, HD), BF16),
            pltpu.VMEM((8, 2 * BLK, HD), BF16),
            pltpu.VMEM((8, 2 * BLK, HD), F32),
            pltpu.VMEM((8, 2 * BLK, HD), BF16),
            pltpu.VMEM((SIDES, HD, ROWS), F32),
            pltpu.SemaphoreType.DMA((SIDES + 1,)),
            pltpu.SemaphoreType.DMA((3,)),
        ],
        compiler_params=room(56),
        cost_estimate=pl.CostEstimate(flops=2_000_000_000, bytes_accessed=8_000_000, transcendentals=2_000_000),
        name="attend",
    )(ids, pairs, *packs, col)


def add_cores_kernel(mine, other, keep, *sends):
    keep[...] = mine[0] + other[0]
    for i, send in enumerate(sends):
        send[...] = (mine[i + 1] + other[i + 1]).astype(BF16)


def add_cores(mine, other):
    return pl.pallas_call(
        add_cores_kernel,
        out_shape=(jax.ShapeDtypeStruct((HD, ROWS), F32),) + (jax.ShapeDtypeStruct((HD, ROWS), BF16),) * 3,
        in_specs=vmem(2),
        out_specs=tuple(vmem(4)),
        cost_estimate=pl.CostEstimate(flops=400_000, bytes_accessed=5_000_000, transcendentals=0),
        compiler_params=room(8),
        name="add_cores",
    )(mine, other)


def query_kernel(a, b, c, d, out):
    total = (a[...] + b[...].astype(F32)) + (c[...].astype(F32) + d[...].astype(F32))
    for h in range(HEADS):
        out[h] = total[:, h * BLK : (h + 1) * BLK].T.astype(BF16)


def finish_query(parts):
    return pl.pallas_call(
        query_kernel,
        out_shape=jax.ShapeDtypeStruct((HEADS, BLK, HD), BF16),
        in_specs=vmem(4),
        out_specs=vmem(1)[0],
        cost_estimate=pl.CostEstimate(flops=60_000_000_000, bytes_accessed=2_000_000, transcendentals=0),
        compiler_params=room(4),
        name="finish_query",
    )(*parts)


def sum_rows_kernel(parts, out):
    total = parts[0].astype(F32)
    for j in range(1, 8):
        total = total + parts[j].astype(F32)
    low = total.astype(BF16)
    for z in range(KVH):
        out[z] = low


def sum_rows(parts):
    return pl.pallas_call(
        sum_rows_kernel,
        out_shape=jax.ShapeDtypeStruct((KVH, 2 * BLK, HD), BF16),
        in_specs=vmem(1),
        out_specs=vmem(1)[0],
        compiler_params=room(4),
        name="sum_rows",
    )(parts)


def split_heads_kernel(parts, key_out, value_out):
    both = parts[...].astype(F32)
    key_out[...] = jnp.swapaxes(both[:, 0:BLK], 0, 1).astype(BF16)
    value_out[...] = jnp.swapaxes(both[:, BLK : 2 * BLK], 0, 1).astype(BF16)


def split_heads(parts):
    return pl.pallas_call(
        split_heads_kernel,
        out_shape=(jax.ShapeDtypeStruct((BLK, KVH, HD), BF16),) * 2,
        in_specs=vmem(1),
        out_specs=tuple(vmem(2)),
        compiler_params=room(4),
        name="split_heads",
    )(parts)


def body(queries, keys, values, outputs, out_grad, log_norm, parents):
    yh, core, x, yl, z = (lax.axis_index(a) for a in ("yh", "core", "x", "yl", "z"))
    kv = jnp.concatenate(
        [lax.dynamic_index_in_dim(keys, z, 1, False), lax.dynamic_index_in_dim(values, z, 1, False)], 0
    )
    ids = [
        16 * yh + 8 * (core if side < 4 else 1 - core) + 2 * ((x + DISTANCES[side % 4]) % 4) + yl
        for side in range(SIDES)
    ]
    ids = jnp.stack([*ids, 8 * core + 2 * x]).astype(jnp.int32)

    queries, out_grad, outputs = (jnp.swapaxes(a, 0, 1) for a in (queries, out_grad, outputs))
    pack = prepare(queries, out_grad, outputs, log_norm)
    pack, kv = lax.optimization_barrier((pack, kv))
    near = [shift(pack, "x", -d) for d in DISTANCES[1:]]
    col = lax.all_to_all(jnp.broadcast_to(kv[None], (8, 2 * BLK, HD)), Y, 0, 0)
    swapped = [shift(pack, "core", 1)]
    ids, near[0], near[1] = lax.optimization_barrier((ids, near[0], near[1]))
    pairs = reach(ids, parents)
    swapped += [shift(p, "core", 1) for p in near]
    packs = [pack, *near, *swapped]
    part, mine, other = attend(ids, pairs, packs, col)
    row = lax.all_to_all(part, Y, 0, 0)
    keep, *sends = add_cores(mine, shift(other, "core", 1))
    got = [shift(g, "x", d) for g, d in zip(sends, DISTANCES[1:], strict=True)]
    row, keep = lax.optimization_barrier((row, keep))
    heads = lax.all_to_all(sum_rows(row), "z", 0, 0)
    query_grad = finish_query([keep, *got])
    key_grad, value_grad = split_heads(heads)
    return jnp.swapaxes(query_grad, 0, 1), key_grad, value_grad


def solution(mesh):
    fine = Mesh(mesh.devices.reshape(4, 2, 4, 2, 8), ("yh", "core", "x", "yl", "z"))
    tokens = ("yh", "core", "x", "yl")
    in_specs = (
        P(tokens, "z", None),
        P(tokens, None, None),
        P(tokens, None, None),
        P(tokens, "z", None),
        P(tokens, "z", None),
        P("z", tokens),
        P(),
    )
    out_specs = (P(tokens, "z", None), P(tokens, None, None), P(tokens, None, None))
    return jax.shard_map(body, mesh=fine, in_specs=in_specs, out_specs=out_specs, check_vma=False)
```

```python
import functools

import jax
import jax.numpy as jnp
from jax import lax
from jax.experimental import pallas as pl
from jax.experimental.pallas import tpu as pltpu
from jax.sharding import Mesh, PartitionSpec as P

BLK = 128
HD = 128
HEADS = 6
ROWS = HEADS * BLK
NBLK = 64
KVH = 8
SIDES = 8
COLUMN = ("yh", "xh")
SQUARE = ("xl", "yl")
STAT_ROWS = 16
PACK_ROWS = 2 * ROWS + 3 * STAT_ROWS
DOTS = 8
SCALING = HD ** -0.5
LOG2E = 1.4426950408889634
PER_STEP = 2
F32 = jnp.float32
BF16 = jnp.bfloat16


def swap_cores(block):
    return lax.ppermute(block, "core", [(0, 1), (1, 0)])


def exchange(block, flip):
    return lax.ppermute(block, SQUARE, [(i, i ^ flip) for i in range(4)])


def room(mebibytes):
    return pltpu.CompilerParams(vmem_limit_bytes=mebibytes * 1024 * 1024)


def vmem(count):
    return [pl.BlockSpec(memory_space=pltpu.VMEM)] * count


def anywhere(count):
    return [pl.BlockSpec(memory_space=pl.ANY)] * count


def smem(count):
    return [pl.BlockSpec(memory_space=pltpu.SMEM)] * count


def reach_kernel(ids, parents, pairs, low, high):
    def step(block, carry):
        above = parents[block]
        root = above == block
        bit = jnp.left_shift(jnp.int32(1), block % 32)
        low[block] = jnp.where(root, 0, low[above]) | jnp.where(block < 32, bit, 0)
        high[block] = jnp.where(root, 0, high[above]) | jnp.where(block < 32, 0, bit)
        return carry

    lax.fori_loop(0, NBLK, step, 0, unroll=True)
    first = ids[SIDES]

    def look(k, count):
        side, j = (k // 8 + 4) % SIDES, k % 8
        block = first + 16 * (j // 2) + 4 * (j % 2)
        mine = ids[side]
        word = jnp.where(block < 32, low[mine], high[mine])
        take = ((jnp.right_shift(word, block % 32) & 1) == 1) & (block != mine)
        pairs[2 + count] = 8 * side + j
        return count + take.astype(jnp.int32)

    others = lax.fori_loop(0, SIDES * 4, look, 0, unroll=True)
    count = lax.fori_loop(SIDES * 4, SIDES * 8, look, others, unroll=True)
    pairs[0] = others
    pairs[1] = count - others
    pairs[2 + count] = 0


def reach(ids, parents):
    return pl.pallas_call(
        reach_kernel,
        out_shape=jax.ShapeDtypeStruct((SIDES * 8 + 3,), jnp.int32),
        in_specs=smem(2),
        out_specs=smem(1)[0],
        scratch_shapes=[pltpu.SMEM((NBLK,), jnp.int32)] * 2,
        cost_estimate=pl.CostEstimate(flops=60_000_000_000, bytes_accessed=1000, transcendentals=0),
        compiler_params=room(1),
        name="reach",
    )(ids, parents)


def prepare_kernel(head, q_hbm, do_hbm, o_hbm, ln_hbm, k_hbm, v_hbm, pack_ref, kv_ref, *scratch):
    q_ref, do_ref, o_ref, ln_ref, k_ref, v_ref, stat, heads, sems = scratch
    routes = (
        (do_hbm, do_ref),
        (o_hbm, o_ref),
        (ln_hbm, ln_ref),
        (q_hbm, q_ref),
        (k_hbm, k_ref),
        (v_hbm, v_ref),
    )
    copies = [pltpu.make_async_copy(src, dst, sems.at[i]) for i, (src, dst) in enumerate(routes)]
    for copy in copies:
        copy.start()
    stat[...] = jnp.zeros_like(stat)
    for copy in copies:
        copy.wait()
    pack_ref[0:ROWS] = q_ref[...].reshape(ROWS, HD)
    pack_ref[ROWS : 2 * ROWS] = do_ref[...].reshape(ROWS, HD)
    stat[0:HEADS] = ln_ref[...]
    for h in range(HEADS):
        prod = do_ref[h].astype(F32) * o_ref[h].astype(F32)
        stat[DOTS + h : DOTS + h + 1] = jnp.sum(prod.T, axis=0, keepdims=True)
    rest = stat[...]
    for part in range(3):
        high = rest.astype(BF16)
        start = 2 * ROWS + part * STAT_ROWS
        pack_ref[start : start + STAT_ROWS] = high
        rest = rest - high.astype(F32)
    for i, ref in enumerate((k_ref, v_ref)):
        heads[...] = jnp.swapaxes(ref[...].astype(F32), 0, 1)
        one = heads[head[0]].astype(BF16)
        for j in range(8):
            kv_ref[j, i * BLK : (i + 1) * BLK] = one


def prepare(head, queries, out_grad, outputs, log_norm, keys, values):
    return pl.pallas_call(
        prepare_kernel,
        out_shape=(
            jax.ShapeDtypeStruct((PACK_ROWS, HD), BF16),
            jax.ShapeDtypeStruct((8, 2 * BLK, HD), BF16),
        ),
        in_specs=smem(1) + anywhere(6),
        out_specs=tuple(vmem(2)),
        scratch_shapes=[pltpu.VMEM((HEADS, BLK, HD), BF16)] * 3
        + [pltpu.VMEM((HEADS, BLK), F32)]
        + [pltpu.VMEM((BLK, KVH, HD), BF16)] * 2
        + [pltpu.VMEM((STAT_ROWS, BLK), F32), pltpu.VMEM((KVH, BLK, HD), F32), pltpu.SemaphoreType.DMA((6,))],
        cost_estimate=pl.CostEstimate(flops=4_000_000, bytes_accessed=1_000_000, transcendentals=0),
        compiler_params=room(60),
        name="prepare",
    )(head, queries, out_grad, outputs, log_norm, keys, values)


NT = (((1,), (1,)), ((), ()))
NN = (((1,), (0,)), ((), ()))


def mm(a, b, dims):
    return lax.dot_general(a, b, dims, preferred_element_type=F32)


def attend_kernel(ids, pairs, *refs):
    remote, (col_hbm, part, mine, other, packs, col, sums, low, both, sems, outs) = refs[:8], refs[8:]
    copies = [pltpu.make_async_copy(remote[side], packs.at[side], sems.at[side]) for side in range(SIDES)]
    copies.append(pltpu.make_async_copy(col_hbm, col, sems.at[SIDES]))
    copies[SIDES].start()
    for copy in copies[:SIDES]:
        copy.start()
    sums[...] = jnp.zeros_like(sums)
    both[...] = jnp.zeros_like(both)

    def visit(work, diagonal=False):
        rows = [
            packs[side, 2 * ROWS : 2 * ROWS + STAT_ROWS].astype(F32)
            + packs[side, 2 * ROWS + STAT_ROWS : 2 * ROWS + 2 * STAT_ROWS].astype(F32)
            + packs[side, 2 * ROWS + 2 * STAT_ROWS : PACK_ROWS].astype(F32)
            for side, _, _ in work
        ]
        norms = [jnp.concatenate([r[h : h + 1] for h in range(HEADS)], 1) * LOG2E for r in rows]
        norms = [n if use is None else jnp.where(use, n, jnp.inf) for n, (_, _, use) in zip(norms, work, strict=True)]
        dots = [jnp.concatenate([r[DOTS + h : DOTS + h + 1] for h in range(HEADS)], 1) for r in rows]
        probs = [
            jnp.exp2(mm(col[j, 0:BLK], packs[side, 0:ROWS], NT) * (SCALING * LOG2E) - norm)
            for (side, j, _), norm in zip(work, norms, strict=True)
        ]
        dprobs = [mm(col[j, BLK : 2 * BLK], packs[side, ROWS : 2 * ROWS], NT) for side, j, _ in work]
        if diagonal:
            token = lax.broadcasted_iota(jnp.int32, (BLK, ROWS), 1) % BLK
            place = lax.broadcasted_iota(jnp.int32, (BLK, ROWS), 0)
            probs = [jnp.where(token >= place, p, 0.0) for p in probs]
        dscores = [(p * (d - dot) * SCALING).astype(BF16) for p, d, dot in zip(probs, dprobs, dots, strict=True)]
        dv = [mm(p.astype(BF16), packs[side, ROWS : 2 * ROWS], NN) for p, (side, _, _) in zip(probs, work, strict=True)]
        dk = [mm(d, packs[side, 0:ROWS], NN) for d, (side, _, _) in zip(dscores, work, strict=True)]
        dq = [mm(col[j, 0:BLK].T, d, NN) for d, (_, j, _) in zip(dscores, work, strict=True)]
        for (side, j, _), k_part, v_part, q_part in zip(work, dk, dv, dq, strict=True):
            sums[j, 0:BLK] += k_part
            sums[j, BLK : 2 * BLK] += v_part
            both[side] += q_part

    own = ids[0]
    copies[SIDES].wait()
    copies[0].wait()
    visit([(0, 2 * (own // 16) + own // 4 % 2, None)], diagonal=True)
    for copy in copies[1:SIDES]:
        copy.wait()

    def visit_all(start, count):
        def step(i, carry):
            work = []
            for k in range(PER_STEP):
                at = PER_STEP * i + k
                code = pairs[start + jnp.minimum(at, count)]
                work.append((code // 8, code % 8, (at < count) if k else None))
            visit(work)
            return carry

        lax.fori_loop(0, (count + PER_STEP - 1) // PER_STEP, step, 0)

    visit_all(2, pairs[0])
    sent = pltpu.make_async_copy(both.at[4:8], other, outs.at[1])
    sent.start()
    visit_all(2 + pairs[0], pairs[1])
    low[...] = sums[...].astype(BF16)
    copies = [pltpu.make_async_copy(low, part, outs.at[0]), pltpu.make_async_copy(both.at[0:4], mine, outs.at[2])]
    for copy in copies:
        copy.start()
    for copy in [sent, *copies]:
        copy.wait()


def attend(ids, pairs, packs, col):
    return pl.pallas_call(
        attend_kernel,
        out_shape=(
            jax.ShapeDtypeStruct((8, 2 * BLK, HD), BF16),
            jax.ShapeDtypeStruct((4, HD, ROWS), F32),
            jax.ShapeDtypeStruct((4, HD, ROWS), F32),
        ),
        in_specs=smem(2) + anywhere(SIDES + 1),
        out_specs=tuple(anywhere(3)),
        scratch_shapes=[
            pltpu.VMEM((SIDES, PACK_ROWS, HD), BF16),
            pltpu.VMEM((8, 2 * BLK, HD), BF16),
            pltpu.VMEM((8, 2 * BLK, HD), F32),
            pltpu.VMEM((8, 2 * BLK, HD), BF16),
            pltpu.VMEM((SIDES, HD, ROWS), F32),
            pltpu.SemaphoreType.DMA((SIDES + 1,)),
            pltpu.SemaphoreType.DMA((3,)),
        ],
        compiler_params=room(56),
        cost_estimate=pl.CostEstimate(flops=2_000_000_000, bytes_accessed=8_000_000, transcendentals=2_000_000),
        name="attend",
    )(ids, pairs, *packs, col)


def add_cores_kernel(mine, other, keep, *sends):
    keep[...] = mine[0] + other[0]
    for i, send in enumerate(sends):
        send[...] = (mine[i + 1] + other[i + 1]).astype(BF16)


def add_cores(mine, other):
    return pl.pallas_call(
        add_cores_kernel,
        out_shape=(jax.ShapeDtypeStruct((HD, ROWS), F32),) + (jax.ShapeDtypeStruct((HD, ROWS), BF16),) * 3,
        in_specs=vmem(2),
        out_specs=tuple(vmem(4)),
        cost_estimate=pl.CostEstimate(flops=400_000, bytes_accessed=5_000_000, transcendentals=0),
        compiler_params=room(8),
        name="add_cores",
    )(mine, other)


def query_kernel(a, b, c, d, out):
    total = (a[...] + b[...].astype(F32)) + (c[...].astype(F32) + d[...].astype(F32))
    for h in range(HEADS):
        out[h] = total[:, h * BLK : (h + 1) * BLK].T.astype(BF16)


def finish_query(parts):
    return pl.pallas_call(
        query_kernel,
        out_shape=jax.ShapeDtypeStruct((HEADS, BLK, HD), BF16),
        in_specs=vmem(4),
        out_specs=vmem(1)[0],
        cost_estimate=pl.CostEstimate(flops=60_000_000_000, bytes_accessed=2_000_000, transcendentals=0),
        compiler_params=room(4),
        name="finish_query",
    )(*parts)


def sum_rows_kernel(parts, out):
    total = parts[0].astype(F32)
    for j in range(1, 8):
        total = total + parts[j].astype(F32)
    low = total.astype(BF16)
    for z in range(KVH):
        out[z] = low


def sum_rows(parts):
    return pl.pallas_call(
        sum_rows_kernel,
        out_shape=jax.ShapeDtypeStruct((KVH, 2 * BLK, HD), BF16),
        in_specs=vmem(1),
        out_specs=vmem(1)[0],
        compiler_params=room(4),
        name="sum_rows",
    )(parts)


def split_heads_kernel(parts, key_out, value_out):
    both = parts[...].astype(F32)
    key_out[...] = jnp.swapaxes(both[:, 0:BLK], 0, 1).astype(BF16)
    value_out[...] = jnp.swapaxes(both[:, BLK : 2 * BLK], 0, 1).astype(BF16)


def split_heads(parts):
    return pl.pallas_call(
        split_heads_kernel,
        out_shape=(jax.ShapeDtypeStruct((BLK, KVH, HD), BF16),) * 2,
        in_specs=vmem(1),
        out_specs=tuple(vmem(2)),
        compiler_params=room(4),
        name="split_heads",
    )(parts)


def body(queries, keys, values, outputs, out_grad, log_norm, parents):
    yh, core, xh, xl, yl, z = (lax.axis_index(a) for a in ("yh", "core", "xh", "xl", "yl", "z"))
    place = 2 * xl + yl
    ids = [
        16 * yh + 8 * (core if side < 4 else 1 - core) + 4 * xh + jnp.bitwise_xor(place, side % 4)
        for side in range(SIDES)
    ]
    ids = jnp.stack([*ids, 8 * core + place]).astype(jnp.int32)

    queries, out_grad, outputs = (jnp.swapaxes(a, 0, 1) for a in (queries, out_grad, outputs))
    head = jnp.reshape(z, (1,)).astype(jnp.int32)
    pack, kv = prepare(head, queries, out_grad, outputs, log_norm, keys, values)
    near = [exchange(pack, flip) for flip in (1, 2, 3)]
    col = lax.all_to_all(kv, COLUMN, 0, 0)
    ids, near[0], near[1], again = lax.optimization_barrier((ids, near[0], near[1], pack))
    pairs = reach(ids, parents)
    swapped = [swap_cores(p) for p in [again, *near]]
    packs = [pack, *near, *swapped]
    part, mine, other = attend(ids, pairs, packs, col)
    row = lax.all_to_all(part, COLUMN, 0, 0)
    keep, *sends = add_cores(mine, swap_cores(other))
    got = [exchange(send, flip) for flip, send in enumerate(sends, 1)]
    row, keep = lax.optimization_barrier((row, keep))
    heads = lax.all_to_all(sum_rows(row), "z", 0, 0)
    query_grad = finish_query([keep, *got])
    key_grad, value_grad = split_heads(heads)
    return jnp.swapaxes(query_grad, 0, 1), key_grad, value_grad


def solution(mesh):
    fine = Mesh(mesh.devices.reshape(4, 2, 2, 2, 2, 8), ("yh", "core", "xh", "xl", "yl", "z"))
    tokens = ("yh", "core", "xh", "xl", "yl")
    in_specs = (
        P(tokens, "z", None),
        P(tokens, None, None),
        P(tokens, None, None),
        P(tokens, "z", None),
        P(tokens, "z", None),
        P("z", tokens),
        P(),
    )
    out_specs = (P(tokens, "z", None), P(tokens, None, None), P(tokens, None, None))
    return jax.shard_map(body, mesh=fine, in_specs=in_specs, out_specs=out_specs, check_vma=False)
```

```python
import functools

import jax
import jax.numpy as jnp
from jax import lax
from jax.experimental import pallas as pl
from jax.experimental.pallas import tpu as pltpu
from jax.sharding import Mesh, PartitionSpec as P

BLK = 128
HD = 128
HEADS = 6
ROWS = HEADS * BLK
NBLK = 64
KVH = 8
SIDES = 8
COLUMN = ("yh", "xh")
SQUARE = ("xl", "yl")
STAT_ROWS = 16
PACK_ROWS = 2 * ROWS + 3 * STAT_ROWS
DOTS = 8
SCALING = HD ** -0.5
LOG2E = 1.4426950408889634
PER_STEP = 2
F32 = jnp.float32
BF16 = jnp.bfloat16


def swap_cores(block):
    return lax.ppermute(block, "core", [(0, 1), (1, 0)])


def exchange(block, flip):
    return lax.ppermute(block, SQUARE, [(i, i ^ flip) for i in range(4)])


def room(mebibytes):
    return pltpu.CompilerParams(vmem_limit_bytes=mebibytes * 1024 * 1024)


def vmem(count):
    return [pl.BlockSpec(memory_space=pltpu.VMEM)] * count


def anywhere(count):
    return [pl.BlockSpec(memory_space=pl.ANY)] * count


def smem(count):
    return [pl.BlockSpec(memory_space=pltpu.SMEM)] * count


def reach_kernel(ids, parents, pairs, low, high):
    def step(block, carry):
        above = parents[block]
        root = above == block
        bit = jnp.left_shift(jnp.int32(1), block % 32)
        low[block] = jnp.where(root, 0, low[above]) | jnp.where(block < 32, bit, 0)
        high[block] = jnp.where(root, 0, high[above]) | jnp.where(block < 32, 0, bit)
        return carry

    lax.fori_loop(0, NBLK, step, 0, unroll=True)
    first = ids[SIDES]

    def look(k, count):
        side, j = (k // 8 + 4) % SIDES, k % 8
        block = first + 16 * (j // 2) + 4 * (j % 2)
        mine = ids[side]
        word = jnp.where(block < 32, low[mine], high[mine])
        take = ((jnp.right_shift(word, block % 32) & 1) == 1) & (block != mine)
        pairs[2 + count] = 8 * side + j
        return count + take.astype(jnp.int32)

    others = lax.fori_loop(0, SIDES * 4, look, 0, unroll=True)
    count = lax.fori_loop(SIDES * 4, SIDES * 8, look, others, unroll=True)
    pairs[0] = others
    pairs[1] = count - others
    pairs[2 + count] = 0


def reach(ids, parents):
    return pl.pallas_call(
        reach_kernel,
        out_shape=jax.ShapeDtypeStruct((SIDES * 8 + 3,), jnp.int32),
        in_specs=smem(2),
        out_specs=smem(1)[0],
        scratch_shapes=[pltpu.SMEM((NBLK,), jnp.int32)] * 2,
        cost_estimate=pl.CostEstimate(flops=60_000_000_000, bytes_accessed=1000, transcendentals=0),
        compiler_params=room(1),
        name="reach",
    )(ids, parents)


def prepare_kernel(head, q_hbm, do_hbm, o_hbm, ln_hbm, k_hbm, v_hbm, pack_ref, kv_ref, *scratch):
    q_ref, do_ref, o_ref, ln_ref, k_ref, v_ref, stat, heads, sems = scratch
    routes = (
        (do_hbm, do_ref),
        (o_hbm, o_ref),
        (ln_hbm, ln_ref),
        (q_hbm, q_ref),
        (k_hbm, k_ref),
        (v_hbm, v_ref),
    )
    copies = [pltpu.make_async_copy(src, dst, sems.at[i]) for i, (src, dst) in enumerate(routes)]
    for copy in copies:
        copy.start()
    stat[...] = jnp.zeros_like(stat)
    for copy in copies:
        copy.wait()
    pack_ref[0:ROWS] = q_ref[...].reshape(ROWS, HD)
    pack_ref[ROWS : 2 * ROWS] = do_ref[...].reshape(ROWS, HD)
    stat[0:HEADS] = ln_ref[...]
    for h in range(HEADS):
        prod = do_ref[h].astype(F32) * o_ref[h].astype(F32)
        stat[DOTS + h : DOTS + h + 1] = jnp.sum(prod.T, axis=0, keepdims=True)
    rest = stat[...]
    for part in range(3):
        high = rest.astype(BF16)
        start = 2 * ROWS + part * STAT_ROWS
        pack_ref[start : start + STAT_ROWS] = high
        rest = rest - high.astype(F32)
    for i, ref in enumerate((k_ref, v_ref)):
        heads[...] = jnp.swapaxes(ref[...].astype(F32), 0, 1)
        one = heads[head[0]].astype(BF16)
        for j in range(8):
            kv_ref[j, i * BLK : (i + 1) * BLK] = one


def prepare(head, queries, out_grad, outputs, log_norm, keys, values):
    return pl.pallas_call(
        prepare_kernel,
        out_shape=(
            jax.ShapeDtypeStruct((PACK_ROWS, HD), BF16),
            jax.ShapeDtypeStruct((8, 2 * BLK, HD), BF16),
        ),
        in_specs=smem(1) + anywhere(6),
        out_specs=tuple(vmem(2)),
        scratch_shapes=[pltpu.VMEM((HEADS, BLK, HD), BF16)] * 3
        + [pltpu.VMEM((HEADS, BLK), F32)]
        + [pltpu.VMEM((BLK, KVH, HD), BF16)] * 2
        + [pltpu.VMEM((STAT_ROWS, BLK), F32), pltpu.VMEM((KVH, BLK, HD), F32), pltpu.SemaphoreType.DMA((6,))],
        cost_estimate=pl.CostEstimate(flops=4_000_000, bytes_accessed=1_000_000, transcendentals=0),
        compiler_params=room(60),
        name="prepare",
    )(head, queries, out_grad, outputs, log_norm, keys, values)


NT = (((1,), (1,)), ((), ()))
NN = (((1,), (0,)), ((), ()))


def mm(a, b, dims):
    return lax.dot_general(a, b, dims, preferred_element_type=F32)


def attend_kernel(ids, pairs, *refs):
    remote, (col_hbm, part, mine, other, packs, col, sums, low, both, sems, outs) = refs[:8], refs[8:]
    copies = [pltpu.make_async_copy(remote[side], packs.at[side], sems.at[side]) for side in range(SIDES)]
    copies.append(pltpu.make_async_copy(col_hbm, col, sems.at[SIDES]))
    copies[SIDES].start()
    for copy in copies[:SIDES]:
        copy.start()
    sums[...] = jnp.zeros_like(sums)
    both[...] = jnp.zeros_like(both)

    def visit(work, diagonal=False):
        rows = [
            packs[side, 2 * ROWS : 2 * ROWS + STAT_ROWS].astype(F32)
            + packs[side, 2 * ROWS + STAT_ROWS : 2 * ROWS + 2 * STAT_ROWS].astype(F32)
            + packs[side, 2 * ROWS + 2 * STAT_ROWS : PACK_ROWS].astype(F32)
            for side, _, _ in work
        ]
        norms = [jnp.concatenate([r[h : h + 1] for h in range(HEADS)], 1) * LOG2E for r in rows]
        norms = [n if use is None else jnp.where(use, n, jnp.inf) for n, (_, _, use) in zip(norms, work, strict=True)]
        dots = [jnp.concatenate([r[DOTS + h : DOTS + h + 1] for h in range(HEADS)], 1) for r in rows]
        probs = [
            jnp.exp2(mm(col[j, 0:BLK], packs[side, 0:ROWS], NT) * (SCALING * LOG2E) - norm)
            for (side, j, _), norm in zip(work, norms, strict=True)
        ]
        dprobs = [mm(col[j, BLK : 2 * BLK], packs[side, ROWS : 2 * ROWS], NT) for side, j, _ in work]
        if diagonal:
            token = lax.broadcasted_iota(jnp.int32, (BLK, ROWS), 1) % BLK
            place = lax.broadcasted_iota(jnp.int32, (BLK, ROWS), 0)
            probs = [jnp.where(token >= place, p, 0.0) for p in probs]
        dscores = [(p * (d - dot) * SCALING).astype(BF16) for p, d, dot in zip(probs, dprobs, dots, strict=True)]
        dv = [mm(p.astype(BF16), packs[side, ROWS : 2 * ROWS], NN) for p, (side, _, _) in zip(probs, work, strict=True)]
        dk = [mm(d, packs[side, 0:ROWS], NN) for d, (side, _, _) in zip(dscores, work, strict=True)]
        dq = [mm(col[j, 0:BLK].T, d, NN) for d, (_, j, _) in zip(dscores, work, strict=True)]
        for (side, j, _), k_part, v_part, q_part in zip(work, dk, dv, dq, strict=True):
            sums[j, 0:BLK] += k_part
            sums[j, BLK : 2 * BLK] += v_part
            both[side] += q_part

    own = ids[0]
    copies[SIDES].wait()
    copies[0].wait()
    visit([(0, 2 * (own // 16) + own // 4 % 2, None)], diagonal=True)
    for copy in copies[1:SIDES]:
        copy.wait()

    def visit_all(start, count):
        def step(i, carry):
            work = []
            for k in range(PER_STEP):
                at = PER_STEP * i + k
                code = pairs[start + jnp.minimum(at, count)]
                work.append((code // 8, code % 8, (at < count) if k else None))
            visit(work)
            return carry

        lax.fori_loop(0, (count + PER_STEP - 1) // PER_STEP, step, 0)

    visit_all(2, pairs[0])
    sent = pltpu.make_async_copy(both.at[4:8], other, outs.at[1])
    sent.start()
    visit_all(2 + pairs[0], pairs[1])
    low[...] = sums[...].astype(BF16)
    copies = [pltpu.make_async_copy(low, part, outs.at[0]), pltpu.make_async_copy(both.at[0:4], mine, outs.at[2])]
    for copy in copies:
        copy.start()
    for copy in [sent, *copies]:
        copy.wait()


def attend(ids, pairs, packs, col):
    return pl.pallas_call(
        attend_kernel,
        out_shape=(
            jax.ShapeDtypeStruct((8, 2 * BLK, HD), BF16),
            jax.ShapeDtypeStruct((4, HD, ROWS), F32),
            jax.ShapeDtypeStruct((4, HD, ROWS), F32),
        ),
        in_specs=smem(2) + anywhere(SIDES + 1),
        out_specs=tuple(anywhere(3)),
        scratch_shapes=[
            pltpu.VMEM((SIDES, PACK_ROWS, HD), BF16),
            pltpu.VMEM((8, 2 * BLK, HD), BF16),
            pltpu.VMEM((8, 2 * BLK, HD), F32),
            pltpu.VMEM((8, 2 * BLK, HD), BF16),
            pltpu.VMEM((SIDES, HD, ROWS), F32),
            pltpu.SemaphoreType.DMA((SIDES + 1,)),
            pltpu.SemaphoreType.DMA((3,)),
        ],
        compiler_params=room(56),
        cost_estimate=pl.CostEstimate(flops=2_000_000_000, bytes_accessed=8_000_000, transcendentals=2_000_000),
        name="attend",
    )(ids, pairs, *packs, col)


def add_cores_kernel(mine, other, keep, *sends):
    keep[...] = mine[0] + other[0]
    for i, send in enumerate(sends):
        send[...] = (mine[i + 1] + other[i + 1]).astype(BF16)


def add_cores(mine, other):
    return pl.pallas_call(
        add_cores_kernel,
        out_shape=(jax.ShapeDtypeStruct((HD, ROWS), F32),) + (jax.ShapeDtypeStruct((HD, ROWS), BF16),) * 3,
        in_specs=vmem(2),
        out_specs=tuple(vmem(4)),
        cost_estimate=pl.CostEstimate(flops=400_000, bytes_accessed=5_000_000, transcendentals=0),
        compiler_params=room(8),
        name="add_cores",
    )(mine, other)


def query_kernel(a, b, c, d, out):
    total = (a[...] + b[...].astype(F32)) + (c[...].astype(F32) + d[...].astype(F32))
    for h in range(HEADS):
        out[h] = total[:, h * BLK : (h + 1) * BLK].T.astype(BF16)


def finish_query(parts):
    return pl.pallas_call(
        query_kernel,
        out_shape=jax.ShapeDtypeStruct((HEADS, BLK, HD), BF16),
        in_specs=vmem(4),
        out_specs=vmem(1)[0],
        cost_estimate=pl.CostEstimate(flops=60_000_000_000, bytes_accessed=2_000_000, transcendentals=0),
        compiler_params=room(4),
        name="finish_query",
    )(*parts)


def sum_rows_kernel(parts, out):
    total = parts[0].astype(F32)
    for j in range(1, 8):
        total = total + parts[j].astype(F32)
    low = total.astype(BF16)
    for z in range(KVH):
        out[z] = low


def sum_rows(parts):
    return pl.pallas_call(
        sum_rows_kernel,
        out_shape=jax.ShapeDtypeStruct((KVH, 2 * BLK, HD), BF16),
        in_specs=vmem(1),
        out_specs=vmem(1)[0],
        compiler_params=room(4),
        name="sum_rows",
    )(parts)


def split_heads_kernel(parts, key_out, value_out):
    both = parts[...].astype(F32)
    key_out[...] = jnp.swapaxes(both[:, 0:BLK], 0, 1).astype(BF16)
    value_out[...] = jnp.swapaxes(both[:, BLK : 2 * BLK], 0, 1).astype(BF16)


def split_heads(parts):
    return pl.pallas_call(
        split_heads_kernel,
        out_shape=(jax.ShapeDtypeStruct((BLK, KVH, HD), BF16),) * 2,
        in_specs=vmem(1),
        out_specs=tuple(vmem(2)),
        compiler_params=room(4),
        name="split_heads",
    )(parts)


def body(queries, keys, values, outputs, out_grad, log_norm, parents):
    yh, core, xh, xl, yl, z = (lax.axis_index(a) for a in ("yh", "core", "xh", "xl", "yl", "z"))
    place = 2 * xl + yl
    ids = [
        16 * yh + 8 * (core if side < 4 else 1 - core) + 4 * xh + jnp.bitwise_xor(place, side % 4)
        for side in range(SIDES)
    ]
    ids = jnp.stack([*ids, 8 * core + place]).astype(jnp.int32)

    queries, out_grad, outputs = (jnp.swapaxes(a, 0, 1) for a in (queries, out_grad, outputs))
    head = jnp.reshape(z, (1,)).astype(jnp.int32)
    pack, kv = prepare(head, queries, out_grad, outputs, log_norm, keys, values)
    near = [exchange(pack, 1), exchange(pack, 2)]
    col = lax.all_to_all(kv, COLUMN, 0, 0)
    ids, near[0], near[1], again = lax.optimization_barrier((ids, near[0], near[1], pack))
    pairs = reach(ids, parents)
    near.append(exchange(near[0], 2))
    swapped = [swap_cores(p) for p in [again, *near[:2]]]
    far, pairs, *swapped = lax.optimization_barrier((near[2], pairs, *swapped))
    swapped.append(swap_cores(far))
    packs = [pack, *near, *swapped]
    part, mine, other = attend(ids, pairs, packs, col)
    row = lax.all_to_all(part, COLUMN, 0, 0)
    keep, *sends = add_cores(mine, swap_cores(other))
    got = [exchange(send, flip) for flip, send in enumerate(sends, 1)]
    row, keep = lax.optimization_barrier((row, keep))
    heads = lax.all_to_all(sum_rows(row), "z", 0, 0)
    query_grad = finish_query([keep, *got])
    key_grad, value_grad = split_heads(heads)
    return jnp.swapaxes(query_grad, 0, 1), key_grad, value_grad


def solution(mesh):
    fine = Mesh(mesh.devices.reshape(4, 2, 2, 2, 2, 8), ("yh", "core", "xh", "xl", "yl", "z"))
    tokens = ("yh", "core", "xh", "xl", "yl")
    in_specs = (
        P(tokens, "z", None),
        P(tokens, None, None),
        P(tokens, None, None),
        P(tokens, "z", None),
        P(tokens, "z", None),
        P("z", tokens),
        P(),
    )
    out_specs = (P(tokens, "z", None), P(tokens, None, None), P(tokens, None, None))
    return jax.shard_map(body, mesh=fine, in_specs=in_specs, out_specs=out_specs, check_vma=False)
```

```python
import functools

import jax
import jax.numpy as jnp
from jax import lax
from jax.experimental import pallas as pl
from jax.experimental.pallas import tpu as pltpu
from jax.sharding import Mesh, PartitionSpec as P

BLK = 128
HD = 128
HEADS = 6
ROWS = HEADS * BLK
NBLK = 64
KVH = 8
SIDES = 8
COLUMN = ("yh", "xh")
SQUARE = ("xl", "yl")
STAT_ROWS = 16
PACK_ROWS = 2 * ROWS + 3 * STAT_ROWS
DOTS = 8
SCALING = HD ** -0.5
LOG2E = 1.4426950408889634
PER_STEP = 2
F32 = jnp.float32
BF16 = jnp.bfloat16


def swap_cores(block):
    return lax.ppermute(block, "core", [(0, 1), (1, 0)])


def exchange(block, flip):
    return lax.ppermute(block, SQUARE, [(i, i ^ flip) for i in range(4)])


def room(mebibytes):
    return pltpu.CompilerParams(vmem_limit_bytes=mebibytes * 1024 * 1024)


def vmem(count):
    return [pl.BlockSpec(memory_space=pltpu.VMEM)] * count


def anywhere(count):
    return [pl.BlockSpec(memory_space=pl.ANY)] * count


def smem(count):
    return [pl.BlockSpec(memory_space=pltpu.SMEM)] * count


def reach_kernel(ids, parents, pairs, low, high):
    def step(block, carry):
        above = parents[block]
        root = above == block
        bit = jnp.left_shift(jnp.int32(1), block % 32)
        low[block] = jnp.where(root, 0, low[above]) | jnp.where(block < 32, bit, 0)
        high[block] = jnp.where(root, 0, high[above]) | jnp.where(block < 32, 0, bit)
        return carry

    lax.fori_loop(0, NBLK, step, 0, unroll=True)
    first = ids[SIDES]

    def look(k, count):
        side, j = (k // 8 + 4) % SIDES, k % 8
        block = first + 16 * (j // 2) + 4 * (j % 2)
        mine = ids[side]
        word = jnp.where(block < 32, low[mine], high[mine])
        take = ((jnp.right_shift(word, block % 32) & 1) == 1) & (block != mine)
        pairs[2 + count] = 8 * side + j
        return count + take.astype(jnp.int32)

    others = lax.fori_loop(0, SIDES * 4, look, 0, unroll=True)
    count = lax.fori_loop(SIDES * 4, SIDES * 8, look, others, unroll=True)
    pairs[0] = others
    pairs[1] = count - others
    pairs[2 + count] = 0


def reach(ids, parents):
    return pl.pallas_call(
        reach_kernel,
        out_shape=jax.ShapeDtypeStruct((SIDES * 8 + 3,), jnp.int32),
        in_specs=smem(2),
        out_specs=smem(1)[0],
        scratch_shapes=[pltpu.SMEM((NBLK,), jnp.int32)] * 2,
        cost_estimate=pl.CostEstimate(flops=60_000_000_000, bytes_accessed=1000, transcendentals=0),
        compiler_params=room(1),
        name="reach",
    )(ids, parents)


def prepare_kernel(head, q_hbm, do_hbm, o_hbm, ln_hbm, k_hbm, v_hbm, pack_ref, kv_ref, *scratch):
    q_ref, do_ref, o_ref, ln_ref, k_ref, v_ref, stat, heads, sems = scratch
    routes = (
        (do_hbm, do_ref),
        (o_hbm, o_ref),
        (ln_hbm, ln_ref),
        (q_hbm, q_ref),
        (k_hbm, k_ref),
        (v_hbm, v_ref),
    )
    copies = [pltpu.make_async_copy(src, dst, sems.at[i]) for i, (src, dst) in enumerate(routes)]
    for copy in copies:
        copy.start()
    stat[...] = jnp.zeros_like(stat)
    for copy in copies:
        copy.wait()
    pack_ref[0:ROWS] = q_ref[...].reshape(ROWS, HD)
    pack_ref[ROWS : 2 * ROWS] = do_ref[...].reshape(ROWS, HD)
    stat[0:HEADS] = ln_ref[...]
    for h in range(HEADS):
        prod = do_ref[h].astype(F32) * o_ref[h].astype(F32)
        stat[DOTS + h : DOTS + h + 1] = jnp.sum(prod.T, axis=0, keepdims=True)
    rest = stat[...]
    for part in range(3):
        high = rest.astype(BF16)
        start = 2 * ROWS + part * STAT_ROWS
        pack_ref[start : start + STAT_ROWS] = high
        rest = rest - high.astype(F32)
    for i, ref in enumerate((k_ref, v_ref)):
        heads[...] = jnp.swapaxes(ref[...].astype(F32), 0, 1)
        one = heads[head[0]].astype(BF16)
        for j in range(8):
            kv_ref[j, i * BLK : (i + 1) * BLK] = one


def prepare(head, queries, out_grad, outputs, log_norm, keys, values):
    return pl.pallas_call(
        prepare_kernel,
        out_shape=(
            jax.ShapeDtypeStruct((PACK_ROWS, HD), BF16),
            jax.ShapeDtypeStruct((8, 2 * BLK, HD), BF16),
        ),
        in_specs=smem(1) + anywhere(6),
        out_specs=tuple(vmem(2)),
        scratch_shapes=[pltpu.VMEM((HEADS, BLK, HD), BF16)] * 3
        + [pltpu.VMEM((HEADS, BLK), F32)]
        + [pltpu.VMEM((BLK, KVH, HD), BF16)] * 2
        + [pltpu.VMEM((STAT_ROWS, BLK), F32), pltpu.VMEM((KVH, BLK, HD), F32), pltpu.SemaphoreType.DMA((6,))],
        cost_estimate=pl.CostEstimate(flops=4_000_000, bytes_accessed=1_000_000, transcendentals=0),
        compiler_params=room(60),
        name="prepare",
    )(head, queries, out_grad, outputs, log_norm, keys, values)


NT = (((1,), (1,)), ((), ()))
NN = (((1,), (0,)), ((), ()))


def mm(a, b, dims):
    return lax.dot_general(a, b, dims, preferred_element_type=F32)


def attend_kernel(ids, pairs, *refs):
    remote, (col_hbm, part, mine, other, packs, col, sums, low, both, sems, outs) = refs[:8], refs[8:]
    copies = [pltpu.make_async_copy(remote[side], packs.at[side], sems.at[side]) for side in range(SIDES)]
    copies.append(pltpu.make_async_copy(col_hbm, col, sems.at[SIDES]))
    copies[SIDES].start()
    for copy in copies[:SIDES]:
        copy.start()
    sums[...] = jnp.zeros_like(sums)
    both[...] = jnp.zeros_like(both)

    def visit(work, diagonal=False):
        rows = [
            packs[side, 2 * ROWS : 2 * ROWS + STAT_ROWS].astype(F32)
            + packs[side, 2 * ROWS + STAT_ROWS : 2 * ROWS + 2 * STAT_ROWS].astype(F32)
            + packs[side, 2 * ROWS + 2 * STAT_ROWS : PACK_ROWS].astype(F32)
            for side, _, _ in work
        ]
        norms = [jnp.concatenate([r[h : h + 1] for h in range(HEADS)], 1) * LOG2E for r in rows]
        norms = [n if use is None else jnp.where(use, n, jnp.inf) for n, (_, _, use) in zip(norms, work, strict=True)]
        dots = [jnp.concatenate([r[DOTS + h : DOTS + h + 1] for h in range(HEADS)], 1) for r in rows]
        probs = [
            jnp.exp2(mm(col[j, 0:BLK], packs[side, 0:ROWS], NT) * (SCALING * LOG2E) - norm)
            for (side, j, _), norm in zip(work, norms, strict=True)
        ]
        dprobs = [mm(col[j, BLK : 2 * BLK], packs[side, ROWS : 2 * ROWS], NT) for side, j, _ in work]
        if diagonal:
            token = lax.broadcasted_iota(jnp.int32, (BLK, ROWS), 1) % BLK
            place = lax.broadcasted_iota(jnp.int32, (BLK, ROWS), 0)
            probs = [jnp.where(token >= place, p, 0.0) for p in probs]
        dscores = [(p * (d - dot) * SCALING).astype(BF16) for p, d, dot in zip(probs, dprobs, dots, strict=True)]
        dv = [mm(p.astype(BF16), packs[side, ROWS : 2 * ROWS], NN) for p, (side, _, _) in zip(probs, work, strict=True)]
        dk = [mm(d, packs[side, 0:ROWS], NN) for d, (side, _, _) in zip(dscores, work, strict=True)]
        dq = [mm(col[j, 0:BLK].T, d, NN) for d, (_, j, _) in zip(dscores, work, strict=True)]
        for (side, j, _), k_part, v_part, q_part in zip(work, dk, dv, dq, strict=True):
            sums[j, 0:BLK] += k_part
            sums[j, BLK : 2 * BLK] += v_part
            both[side] += q_part

    own = ids[0]
    copies[SIDES].wait()
    copies[0].wait()
    visit([(0, 2 * (own // 16) + own // 4 % 2, None)], diagonal=True)
    for copy in copies[1:SIDES]:
        copy.wait()

    def visit_all(start, count):
        def step(i, carry):
            work = []
            for k in range(PER_STEP):
                at = PER_STEP * i + k
                code = pairs[start + jnp.minimum(at, count)]
                work.append((code // 8, code % 8, (at < count) if k else None))
            visit(work)
            return carry

        lax.fori_loop(0, (count + PER_STEP - 1) // PER_STEP, step, 0)

    visit_all(2, pairs[0])
    sent = pltpu.make_async_copy(both.at[4:8], other, outs.at[1])
    sent.start()
    visit_all(2 + pairs[0], pairs[1])
    low[...] = sums[...].astype(BF16)
    copies = [pltpu.make_async_copy(low, part, outs.at[0]), pltpu.make_async_copy(both.at[0:4], mine, outs.at[2])]
    for copy in copies:
        copy.start()
    for copy in [sent, *copies]:
        copy.wait()


def attend(ids, pairs, packs, col):
    return pl.pallas_call(
        attend_kernel,
        out_shape=(
            jax.ShapeDtypeStruct((8, 2 * BLK, HD), BF16),
            jax.ShapeDtypeStruct((4, HD, ROWS), F32),
            jax.ShapeDtypeStruct((4, HD, ROWS), F32),
        ),
        in_specs=smem(2) + anywhere(SIDES + 1),
        out_specs=tuple(anywhere(3)),
        scratch_shapes=[
            pltpu.VMEM((SIDES, PACK_ROWS, HD), BF16),
            pltpu.VMEM((8, 2 * BLK, HD), BF16),
            pltpu.VMEM((8, 2 * BLK, HD), F32),
            pltpu.VMEM((8, 2 * BLK, HD), BF16),
            pltpu.VMEM((SIDES, HD, ROWS), F32),
            pltpu.SemaphoreType.DMA((SIDES + 1,)),
            pltpu.SemaphoreType.DMA((3,)),
        ],
        compiler_params=room(56),
        cost_estimate=pl.CostEstimate(flops=2_000_000_000, bytes_accessed=8_000_000, transcendentals=2_000_000),
        name="attend",
    )(ids, pairs, *packs, col)


def add_cores_kernel(mine, other, keep, *sends):
    keep[...] = mine[0] + other[0]
    for i, send in enumerate(sends):
        send[...] = (mine[i + 1] + other[i + 1]).astype(BF16)


def add_cores(mine, other):
    return pl.pallas_call(
        add_cores_kernel,
        out_shape=(jax.ShapeDtypeStruct((HD, ROWS), F32),) + (jax.ShapeDtypeStruct((HD, ROWS), BF16),) * 3,
        in_specs=vmem(2),
        out_specs=tuple(vmem(4)),
        cost_estimate=pl.CostEstimate(flops=400_000, bytes_accessed=5_000_000, transcendentals=0),
        compiler_params=room(8),
        name="add_cores",
    )(mine, other)


def query_kernel(a, b, c, d, out):
    total = (a[...] + b[...].astype(F32)) + (c[...].astype(F32) + d[...].astype(F32))
    for h in range(HEADS):
        out[h] = total[:, h * BLK : (h + 1) * BLK].T.astype(BF16)


def finish_query(parts):
    return pl.pallas_call(
        query_kernel,
        out_shape=jax.ShapeDtypeStruct((HEADS, BLK, HD), BF16),
        in_specs=vmem(4),
        out_specs=vmem(1)[0],
        cost_estimate=pl.CostEstimate(flops=60_000_000_000, bytes_accessed=2_000_000, transcendentals=0),
        compiler_params=room(4),
        name="finish_query",
    )(*parts)


def sum_rows_kernel(parts, out):
    total = parts[0].astype(F32)
    for j in range(1, 8):
        total = total + parts[j].astype(F32)
    low = total.astype(BF16)
    for z in range(KVH):
        out[z] = low


def sum_rows(parts):
    return pl.pallas_call(
        sum_rows_kernel,
        out_shape=jax.ShapeDtypeStruct((KVH, 2 * BLK, HD), BF16),
        in_specs=vmem(1),
        out_specs=vmem(1)[0],
        compiler_params=room(4),
        name="sum_rows",
    )(parts)


def split_heads_kernel(parts, key_out, value_out):
    both = parts[...].astype(F32)
    key_out[...] = jnp.swapaxes(both[:, 0:BLK], 0, 1).astype(BF16)
    value_out[...] = jnp.swapaxes(both[:, BLK : 2 * BLK], 0, 1).astype(BF16)


def split_heads(parts):
    return pl.pallas_call(
        split_heads_kernel,
        out_shape=(jax.ShapeDtypeStruct((BLK, KVH, HD), BF16),) * 2,
        in_specs=vmem(1),
        out_specs=tuple(vmem(2)),
        compiler_params=room(4),
        name="split_heads",
    )(parts)


def body(queries, keys, values, outputs, out_grad, log_norm, parents):
    yh, core, xh, xl, yl, z = (lax.axis_index(a) for a in ("yh", "core", "xh", "xl", "yl", "z"))
    place = 2 * xl + yl
    ids = [
        16 * yh + 8 * (core if side < 4 else 1 - core) + 4 * xh + jnp.bitwise_xor(place, side % 4)
        for side in range(SIDES)
    ]
    ids = jnp.stack([*ids, 8 * core + place]).astype(jnp.int32)

    queries, out_grad, outputs = (jnp.swapaxes(a, 0, 1) for a in (queries, out_grad, outputs))
    head = jnp.reshape(z, (1,)).astype(jnp.int32)
    pack, kv = prepare(head, queries, out_grad, outputs, log_norm, keys, values)
    near = [exchange(pack, flip) for flip in (1, 2, 3)]
    col = lax.all_to_all(kv, COLUMN, 0, 0)
    ids, near[0], near[1], again = lax.optimization_barrier((ids, near[0], near[1], pack))
    pairs = reach(ids, parents)
    swapped = [swap_cores(p) for p in [again, *near[:2]]]
    far, pairs, *swapped = lax.optimization_barrier((near[2], pairs, *swapped))
    swapped.append(swap_cores(far))
    packs = [pack, *near, *swapped]
    part, mine, other = attend(ids, pairs, packs, col)
    row = lax.all_to_all(part, COLUMN, 0, 0)
    keep, *sends = add_cores(mine, swap_cores(other))
    got = [exchange(send, flip) for flip, send in enumerate(sends, 1)]
    row, keep = lax.optimization_barrier((row, keep))
    heads = lax.all_to_all(sum_rows(row), "z", 0, 0)
    query_grad = finish_query([keep, *got])
    key_grad, value_grad = split_heads(heads)
    return jnp.swapaxes(query_grad, 0, 1), key_grad, value_grad


def solution(mesh):
    fine = Mesh(mesh.devices.reshape(4, 2, 2, 2, 2, 8), ("yh", "core", "xh", "xl", "yl", "z"))
    tokens = ("yh", "core", "xh", "xl", "yl")
    in_specs = (
        P(tokens, "z", None),
        P(tokens, None, None),
        P(tokens, None, None),
        P(tokens, "z", None),
        P(tokens, "z", None),
        P("z", tokens),
        P(),
    )
    out_specs = (P(tokens, "z", None), P(tokens, None, None), P(tokens, None, None))
    return jax.shard_map(body, mesh=fine, in_specs=in_specs, out_specs=out_specs, check_vma=False)
```
